128 devices in a mesh: energy: 32 (over y, z, x_lo), elem: 4 (over x_hi, core).
Axes of the slice: x: 4 (x_hi: 2, x_lo: 2; x = x_hi * 2 + x_lo), y: 4, z: 4, core: 2. Of those that a mesh axis runs over, the one named last changes fastest.
Arguments:
- g_lesser: bfloat16 [2048, 2, 8192], P('energy', None, 'elem'), may hold values from -6 to 6
- g_greater: bfloat16 [2048, 2, 8192], P('energy', None, 'elem'), may hold values from -6 to 6
- partner: int32 [4, 32, 64], P('elem'), may hold values from 0 to 8191, as said below
Outputs:
- p_lesser: float32 [2048, 2, 8192], P('energy', None, 'elem')
- p_greater: float32 [2048, 2, 8192], P('energy', None, 'elem')
The draws below stay inside these ranges and needn't reach their ends.
Inputs may be any that keep to these rules, and one draw needn't show every extreme that they name: partner[l, e, k] is the flat index (l2 * 32 + e) * 64 + k2 of pair k2 of block (l2, e), where l2 is l with its lowest bit flipped; the map of flat pair indices is an involution (each pair's partner has it as partner).
All inputs are finite; a program needn't handle non-finite values.
Results may differ from the reference program's by a relative error of at most 0.0093.
Values may be sent and summed in bfloat16 or wider, within the bound.
A program may use at most 192 MiB of HBM per device.

```python
import math
import jax
import jax.numpy as jnp
from jax import lax

NE = 2048
NT = 4096
RADIX = 64
OUTER = 64
SPAN = 32
PAIR_DEV = 64
PAIRS = 8192
N_ENERGY = 32
N_ELEM = 4


def draw_partner(key, part):
    key = jax.random.fold_in(key, 7)
    halves = N_ELEM // 2
    subkeys = jax.random.split(key, halves * N_ENERGY)
    shuffles = jax.vmap(lambda subkey: jax.random.permutation(subkey, PAIR_DEV))(subkeys)
    shuffles = shuffles.reshape(halves, N_ENERGY, PAIR_DEV).astype(jnp.int32)
    inverse = jnp.argsort(shuffles, axis=-1).astype(jnp.int32)
    first_block = jnp.arange(halves, dtype=jnp.int32)[:, None, None] * 2
    energy_block = jnp.arange(N_ENERGY, dtype=jnp.int32)[None, :, None]
    to_upper = ((first_block + 1) * N_ENERGY + energy_block) * PAIR_DEV + shuffles
    to_lower = (first_block * N_ENERGY + energy_block) * PAIR_DEV + inverse
    return jnp.stack([to_upper, to_lower], axis=1).reshape(N_ELEM, N_ENERGY, PAIR_DEV)


def block_levels(rng, dims, cuts, low, largest):
    def one(dim, shards_of):
        steps = jax.random.uniform(jax.random.fold_in(jax.random.fold_in(rng, 6), dim), (shards_of,), jnp.float32, low / len(cuts), largest / len(cuts))
        return jnp.repeat(jnp.exp(steps), dims[dim] // shards_of).reshape((-1,) + (1,) * (len(dims) - dim - 1))

    level = one(*cuts[0])
    for cut in cuts[1:]:
        level = level * one(*cut)
    return level


def gaussian(rng, dims, spread, most, shards=(), kind=jnp.bfloat16):
    values = jax.random.normal(rng, dims, jnp.float32) * spread
    if len(shards) > 0:
        values = block_levels(rng, dims, shards, -0.22, 0.18) * values
    return jnp.clip(values, min=-most, max=most).astype(kind)


def setup_inputs(seed: int = 0) -> dict:
    seeds = jax.random.split(jax.random.key(seed), 4)
    g_lesser = gaussian(seeds[0], (NE, 2, PAIRS), 1.0, 6.0, ((0, 32), (2, 4)))
    g_greater = gaussian(seeds[1], (NE, 2, PAIRS), 1.0, 6.0, ((0, 32), (2, 4)))
    partner = draw_partner(jax.random.fold_in(seeds[3], 71), 0)
    return dict(g_lesser=g_lesser, g_greater=g_greater, partner=partner)


def angle_table(rows_count, cols_count, length):
    left = jnp.arange(rows_count, dtype=jnp.int32)[:, None]
    right = jnp.arange(cols_count, dtype=jnp.int32)[None, :]
    phase = left * right % length
    theta = phase.astype(jnp.float32) * (2.0 * math.pi / length)
    return (jnp.cos(theta), jnp.sin(theta))

def make_tables():
    outer_cos, outer_sin = angle_table(OUTER, SPAN, OUTER)
    inner_cos, inner_sin = angle_table(RADIX, RADIX, RADIX)
    twiddle_cos, twiddle_sin = angle_table(OUTER, RADIX, NT)
    return (outer_cos.astype(jnp.bfloat16), outer_sin.astype(jnp.bfloat16), inner_cos.astype(jnp.bfloat16), inner_sin.astype(jnp.bfloat16), twiddle_cos, twiddle_sin)

def mult(form, left, right):
    return jnp.einsum(form, left.astype(jnp.float32), right.astype(jnp.float32), precision=lax.Precision.HIGHEST)

def forward(tables, stacked):
    outer_cos, outer_sin, inner_cos, inner_sin, twiddle_cos, twiddle_sin = tables
    shape = stacked.shape
    real_in = stacked[:, :, 0].reshape(SPAN, RADIX, -1)
    imag_in = stacked[:, :, 1].reshape(SPAN, RADIX, -1)
    y_real = mult('kn,nmc->kmc', outer_cos, real_in) + mult('kn,nmc->kmc', outer_sin, imag_in)
    y_imag = mult('kn,nmc->kmc', outer_cos, imag_in) - mult('kn,nmc->kmc', outer_sin, real_in)
    tw_cos = twiddle_cos[:, :, None]
    tw_sin = twiddle_sin[:, :, None]
    z_real = (tw_cos * y_real + tw_sin * y_imag).astype(jnp.bfloat16)
    z_imag = (tw_cos * y_imag - tw_sin * y_real).astype(jnp.bfloat16)
    t_real = mult('jm,kmc->jkc', inner_cos, z_real) + mult('jm,kmc->jkc', inner_sin, z_imag)
    t_imag = mult('jm,kmc->jkc', inner_cos, z_imag) - mult('jm,kmc->jkc', inner_sin, z_real)
    real_part = t_real.reshape(NT, shape[1], shape[3])
    imag_part = t_imag.reshape(NT, shape[1], shape[3])
    return jnp.stack([real_part, imag_part], axis=2).astype(jnp.bfloat16)

def reverse_time(values):
    return jnp.concatenate([values[:1], values[:0:-1]], axis=0)

def complex_product(own_part, other_part):
    own_f = own_part.astype(jnp.float32)
    other_f = other_part.astype(jnp.float32)
    real_part = own_f[:, :, 0] * other_f[:, :, 0] - own_f[:, :, 1] * other_f[:, :, 1]
    imag_part = own_f[:, :, 0] * other_f[:, :, 1] + own_f[:, :, 1] * other_f[:, :, 0]
    return jnp.stack([real_part, imag_part], axis=2).astype(jnp.bfloat16)

def inverse(tables, products):
    outer_cos, outer_sin, inner_cos, inner_sin, twiddle_cos, twiddle_sin = tables
    shape = products.shape
    real_in = products[:, :, 0].reshape(RADIX, OUTER, -1)
    imag_in = products[:, :, 1].reshape(RADIX, OUTER, -1)
    a_real = mult('jm,jkc->mkc', inner_cos, real_in) - mult('jm,jkc->mkc', inner_sin, imag_in)
    a_imag = mult('jm,jkc->mkc', inner_cos, imag_in) + mult('jm,jkc->mkc', inner_sin, real_in)
    tw_cos = twiddle_cos.T[:, :, None]
    tw_sin = twiddle_sin.T[:, :, None]
    b_real = (tw_cos * a_real - tw_sin * a_imag).astype(jnp.bfloat16)
    b_imag = (tw_cos * a_imag + tw_sin * a_real).astype(jnp.bfloat16)
    x_real = mult('kn,mkc->nmc', outer_cos, b_real) - mult('kn,mkc->nmc', outer_sin, b_imag)
    x_imag = mult('kn,mkc->nmc', outer_cos, b_imag) + mult('kn,mkc->nmc', outer_sin, b_real)
    x_real = x_real.reshape(NE, shape[1], shape[3])
    x_imag = x_imag.reshape(NE, shape[1], shape[3])
    factor = 1.0 / (NT * math.sqrt(NE))
    return jnp.stack([factor * x_imag, -factor * x_real], axis=2)

def reference(g_lesser, g_greater, partner):
    tables = make_tables()
    stacked = jnp.stack([g_lesser, g_greater], axis=1)
    spectra = forward(tables, stacked)
    mates = jnp.take(spectra, partner.reshape(-1), axis=3)[:, ::-1]
    products = complex_product(spectra, reverse_time(mates))
    result = inverse(tables, products)
    return (result[:, 0], result[:, 1])
```

```python
import functools
import math

import jax
import jax.numpy as jnp
import ml_dtypes
import numpy as np
from jax import lax
from jax.experimental import pallas as pl
from jax.experimental.pallas import tpu as pltpu
from jax.sharding import PartitionSpec as P

NE = 2048
NT = 4096
MESH = pl.DeviceIdType.MESH
BF16 = ml_dtypes.bfloat16


def rotation(rows, cols, length, sign):
    theta = np.outer(rows, cols) % length * (2.0 * math.pi / length)
    cos, sin = np.cos(theta), sign * np.sin(theta)
    return np.stack([np.stack([cos, -sin], -1), np.stack([sin, cos], -1)], 1)


def widen(small):
    a, _, b, _ = small.shape
    full = np.einsum("acbd,rs->acrbds", small, np.eye(8))
    return full.reshape(a * 16, b * 16).astype(BF16)


@functools.cache
def constants():
    n = np.arange(64)
    half = np.arange(32)
    k1 = np.stack([widen(rotation(n, half, 64, s)) for s in (-1, 1)])
    a2 = []
    for s in (-1, 1):
        m = rotation(n, n, 64, s).transpose(1, 0, 2, 3).reshape(2, 64, 8, 8, 2)
        a2.append(m.transpose(0, 1, 2, 4, 3).reshape(128, 128))
    a2 = np.stack(a2).astype(BF16)
    b3 = []
    for s in (1, -1):
        m = rotation(n, n, 64, s).reshape(8, 8, 2, 64, 2)
        b3.append(m.transpose(0, 2, 1, 4, 3).reshape(128, 128))
    b3 = np.concatenate(b3).astype(BF16)
    k4 = []
    for s in (1, -1):
        m = rotation(half, n, 64, s)
        m = np.stack([m[:, 1], -m[:, 0]], 1)
        k4.append(widen(m))
    k4 = np.stack(k4)
    theta = np.outer(n, n) * (2.0 * math.pi / NT)
    tw = np.stack([np.cos(theta), np.sin(theta)])
    t1 = tw.reshape(2, 64, 2, 2, 2, 8).transpose(0, 2, 1, 5, 3, 4)
    t1 = np.repeat(t1.reshape(2, 2, 512, 4), 64, axis=3).astype(np.float32)
    t3 = tw / (NT * math.sqrt(NE))
    t3 = t3.reshape(2, 16, 4, 64).transpose(0, 1, 3, 2)
    t3 = np.repeat(t3, 64, axis=3).astype(np.float32)
    out_row = np.arange(256).reshape(8, 16, 2).transpose(1, 2, 0).reshape(-1)
    pi = np.zeros((256, 256))
    pi[np.arange(256), out_row] = 1.0
    return dict(k1=k1, a2=a2, b3=b3, k4=k4, t1=t1, t3=t3, pi=pi.astype(BF16))


def dot(a, b):
    return jnp.dot(a, b, preferred_element_type=jnp.float32)


def swap_halves(first, second):
    width = first.shape[-1]
    axis = first.ndim - 1
    low_parts, high_parts = [], []
    for start in range(0, width, 128):
        a = first[..., start : start + 128]
        b = second[..., start : start + 128]
        lane = lax.broadcasted_iota(jnp.int32, a.shape, axis)
        low_parts.append(jnp.where(lane < 64, a, pltpu.roll(b, 64, axis)))
        high_parts.append(jnp.where(lane < 64, pltpu.roll(a, 64, axis), b))
    if len(low_parts) == 1:
        return low_parts[0], high_parts[0]
    return jnp.concatenate(low_parts, axis), jnp.concatenate(high_parts, axis)


def main_kernel(
    n,
    vl, vg, part, pi_h, k1_h, a2_h, b3_h, k4_h, t1_h, t3_h,
    q_ref,
    x_in, send, recv, zz, bb, outs,
    pi, k1, a2, b3, k4, t1, t3,
    in_sem, const_sem, send_sem, recv_sem, back_send_sem, back_recv_sem,
):
    e = lax.axis_index("energy")
    l = lax.axis_index("elem")
    other = l + 1 - 2 * lax.rem(l, 2)
    barrier = pltpu.get_barrier_semaphore()

    loads = [
        pltpu.make_async_copy(pi_h, pi, const_sem.at[0]),
        pltpu.make_async_copy(vl, x_in.at[0], in_sem.at[0]),
        pltpu.make_async_copy(vg, x_in.at[1], in_sem.at[1]),
    ]
    for copy in loads:
        copy.start()

    def greet(i, carry):
        dst = lax.rem(e + i, n)
        pl.semaphore_signal(barrier, inc=1, device_id=(dst, l), device_id_type=MESH)
        return carry

    def greet_other(i, carry):
        dst = lax.rem(e + i, n)
        pl.semaphore_signal(barrier, inc=1, device_id=(dst, other), device_id_type=MESH)
        return carry

    lax.fori_loop(1, n, greet, 0)
    lax.fori_loop(0, n, greet_other, 0)

    consts = [
        pltpu.make_async_copy(src, dst, const_sem.at[i + 1])
        for i, (src, dst) in enumerate(
            ((k1_h, k1), (t1_h, t1), (a2_h, a2), (b3_h, b3), (t3_h, t3), (k4_h, k4))
        )
    ]
    for copy in consts:
        copy.start()

    def pack(arr):
        for gh in range(4):
            base = gh * 512
            rhs = jnp.concatenate(
                [x_in[arr, base : base + 256, :], x_in[arr, base + 256 : base + 512, :]], axis=1
            )
            rows = dot(pi[...], rhs)
            even, odd = swap_halves(rows[:, :128], rows[:, 128:])
            at = slice(gh * 16, gh * 16 + 16)
            send[arr, :, 0, at, :] = even.reshape(16, 16, 128).astype(jnp.bfloat16)
            send[arr, :, 1, at, :] = odd.reshape(16, 16, 128).astype(jnp.bfloat16)

    def out_copy(arr, dst, elem):
        return pltpu.make_async_remote_copy(
            src_ref=send.at[arr, lax.div(dst, 2), lax.rem(dst, 2)],
            dst_ref=recv.at[arr, e],
            send_sem=send_sem.at[arr],
            recv_sem=recv_sem.at[arr],
            device_id=(dst, elem),
            device_id_type=MESH,
        )

    loads[0].wait()
    loads[1].wait()
    pack(0)
    pl.semaphore_wait(barrier, 2 * n - 1)

    def send_lesser(i, carry):
        out_copy(0, lax.rem(e + i, n), l).start()
        return carry

    def send_greater(i, carry):
        out_copy(1, lax.rem(e + i, n), other).start()
        return carry

    lax.fori_loop(1, n, send_lesser, 0)
    pltpu.make_async_copy(
        send.at[0, lax.div(e, 2), lax.rem(e, 2)], recv.at[0, e], recv_sem.at[0]
    ).start()
    loads[2].wait()
    pack(1)
    lax.fori_loop(0, n, send_greater, 0)

    row = part[pl.ds(e, 1), :] & 63
    row = jnp.concatenate([row, row + 64], axis=1)
    one_hot = jnp.where(lax.broadcasted_iota(jnp.int32, (128, 128), 0) == row, 1.0, 0.0)
    one_hot = one_hot.astype(jnp.bfloat16)

    consts[0].wait()
    consts[1].wait()

    for arr in range(2):
        pltpu.make_async_copy(recv.at[arr], recv.at[arr], recv_sem.at[arr]).wait()
        sign = 1.0 if arr == 0 else -1.0
        for gp in range(2):
            sides = []
            for gh in (2 * gp, 2 * gp + 1):
                side = recv[arr, :, gh * 16 : gh * 16 + 16, :].reshape(512, 128)
                if arr == 1:
                    side = dot(side, one_hot).astype(jnp.bfloat16)
                sides.append(side)
            rhs = jnp.concatenate(sides, axis=1)
            for m in range(4):
                y = dot(k1[arr, m * 256 : (m + 1) * 256, :], rhs).reshape(16, 2, 8, 256)
                y_re, y_im = y[:, 0], y[:, 1]
                cos = t1[0, gp, m * 128 : (m + 1) * 128, :].reshape(16, 8, 256)
                sin = t1[1, gp, m * 128 : (m + 1) * 128, :].reshape(16, 8, 256) * sign
                z_re = cos * y_re + sin * y_im
                z_im = cos * y_im - sin * y_re
                z = jnp.stack([z_re, z_im], axis=1).reshape(8, 2, 16, 256)
                low, high = swap_halves(z[:, 0], z[:, 1])
                low, high = low.astype(jnp.bfloat16), high.astype(jnp.bfloat16)
                for side in range(2):
                    lanes = slice(side * 128, side * 128 + 128)
                    g = 4 * gp + 2 * side
                    zz[arr, m * 8 : m * 8 + 8, g * 16 : g * 16 + 16, :] = low[..., lanes]
                    zz[arr, m * 8 : m * 8 + 8, g * 16 + 16 : g * 16 + 32, :] = high[..., lanes]

    for copy in consts[2:5]:
        copy.wait()

    def middle(j, carry):
        def spectrum(arr):
            rhs = jnp.concatenate([zz[arr, 2 * j], zz[arr, 2 * j + 1]], axis=1)
            return dot(a2[arr], rhs)

        one, two = spectrum(0), spectrum(1)
        l_re, l_im, g_re, g_im = one[:64], one[64:], two[:64], two[64:]
        prod = jnp.concatenate([l_re * g_re - l_im * g_im, l_re * g_im + l_im * g_re], axis=0)
        a = dot(b3[...], prod.astype(jnp.bfloat16)).reshape(2, 8, 2, 8, 256)
        cos = t3[0, j].reshape(8, 8, 256)
        sin = t3[1, j].reshape(8, 8, 256)
        for path, s in ((0, sin), (1, -sin)):
            a_re, a_im = a[path, :, 0], a[path, :, 1]
            b_re = cos * a_re - s * a_im
            b_im = cos * a_im + s * a_re
            b = jnp.stack([b_re, b_im], axis=1).reshape(4, 2, 16, 256)
            low, high = swap_halves(b[:, 0], b[:, 1])
            low, high = low.astype(jnp.bfloat16), high.astype(jnp.bfloat16)
            for side in range(2):
                lanes = slice(side * 128, side * 128 + 128)
                k2 = 4 * j + 2 * side
                bb[path, :, k2, :, :] = low[..., lanes]
                bb[path, :, k2 + 1, :, :] = high[..., lanes]
        return carry

    lax.fori_loop(0, 16, middle, 0)
    consts[5].wait()

    def back_copy(path, dst, elem):
        return pltpu.make_async_remote_copy(
            src_ref=outs.at[path, dst],
            dst_ref=q_ref.at[path, e],
            send_sem=back_send_sem.at[path],
            recv_sem=back_recv_sem.at[path],
            device_id=(dst, elem),
            device_id_type=MESH,
        )

    def back_lesser(i, carry):
        back_copy(0, lax.rem(e + i, n), l).start()
        return carry

    def back_greater(i, carry):
        back_copy(1, lax.rem(e + i, n), other).start()
        return carry

    for path in range(2):
        for gp in range(2):
            rhs = jnp.concatenate(
                [bb[path, 2 * gp].reshape(1024, 128), bb[path, 2 * gp + 1].reshape(1024, 128)],
                axis=1,
            )
            for m in range(2):
                x = dot(k4[path, m * 256 : (m + 1) * 256, :], rhs).astype(jnp.bfloat16)
                for side in range(2):
                    part_x = x[:, side * 128 : side * 128 + 128]
                    if path == 1:
                        part_x = lax.dot_general(
                            part_x, one_hot, (((1,), (1,)), ((), ())), preferred_element_type=jnp.float32
                        ).astype(jnp.bfloat16)
                    gh = 2 * gp + side
                    outs[path, m * 16 : m * 16 + 16, gh * 16 : gh * 16 + 16, :] = part_x.reshape(
                        16, 16, 128
                    )
        if path == 0:
            lax.fori_loop(1, n, back_lesser, 0)
            pltpu.make_async_copy(outs.at[0, e], q_ref.at[0, e], back_recv_sem.at[0]).start()
        else:
            lax.fori_loop(0, n, back_greater, 0)

    for path in range(2):
        pltpu.make_async_copy(q_ref.at[path], q_ref.at[path], back_recv_sem.at[path]).wait()
    for arr in range(2):
        count = n - 1 + arr
        sent = outs.at[arr, pl.ds(0, count)]
        pltpu.make_async_copy(sent, sent, send_sem.at[arr]).wait()
        pltpu.make_async_copy(sent, sent, back_send_sem.at[arr]).wait()


def post_kernel(q, pi_t, lesser, greater):
    for path, out in ((0, lesser), (1, greater)):
        for gh in range(4):
            at = slice(gh * 16, gh * 16 + 16)
            even = q[path, :, 0, at, :].reshape(256, 128)
            odd = q[path, :, 1, at, :].reshape(256, 128)
            rows = dot(pi_t[...], jnp.concatenate([even, odd], axis=1))
            first, second = swap_halves(rows[:, :128], rows[:, 128:])
            out[gh * 512 : gh * 512 + 256, :] = first
            out[gh * 512 + 256 : gh * 512 + 512, :] = second


def as_rows(g):
    return g.reshape(64, 2, 16, 128).transpose(0, 2, 1, 3).reshape(2048, 128)


def from_rows(v):
    return v.reshape(64, 16, 2, 128).transpose(0, 2, 1, 3).reshape(64, 2, 2048)


def per_device(g_lesser, g_greater, partner):
    n = lax.axis_size("energy")
    c = constants()
    any_spec = pl.BlockSpec(memory_space=pl.ANY)
    vmem = pl.BlockSpec(memory_space=pltpu.VMEM)
    names = ("pi", "k1", "a2", "b3", "k4", "t1", "t3")
    tables = [jnp.asarray(c[name]) for name in names]
    scratch = [
        pltpu.VMEM((2, 2048, 128), jnp.bfloat16),
        pltpu.VMEM((2, 16, 2, 64, 128), jnp.bfloat16),
        pltpu.VMEM((2, 32, 64, 128), jnp.bfloat16),
        pltpu.VMEM((2, 32, 128, 128), jnp.bfloat16),
        pltpu.VMEM((2, 4, 64, 16, 128), jnp.bfloat16),
        pltpu.VMEM((2, 32, 64, 128), jnp.bfloat16),
    ]
    scratch += [pltpu.VMEM(t.shape, t.dtype) for t in tables]
    scratch += [
        pltpu.SemaphoreType.DMA((2,)),
        pltpu.SemaphoreType.DMA((7,)),
        pltpu.SemaphoreType.DMA((2,)),
        pltpu.SemaphoreType.DMA((2,)),
        pltpu.SemaphoreType.DMA((2,)),
        pltpu.SemaphoreType.DMA((2,)),
    ]
    q = pl.pallas_call(
        functools.partial(main_kernel, n),
        out_shape=jax.ShapeDtypeStruct((2, 32, 64, 128), jnp.bfloat16),
        in_specs=[any_spec, any_spec, vmem] + [any_spec] * 7,
        out_specs=any_spec,
        scratch_shapes=scratch,
        compiler_params=pltpu.CompilerParams(
            collective_id=0, has_side_effects=True, vmem_limit_bytes=48 * 1024 * 1024
        ),
    )(as_rows(g_lesser), as_rows(g_greater), partner[0], *tables)
    lesser, greater = pl.pallas_call(
        post_kernel,
        out_shape=[jax.ShapeDtypeStruct((2048, 128), jnp.float32)] * 2,
        in_specs=[vmem, vmem],
        out_specs=[vmem, vmem],
        compiler_params=pltpu.CompilerParams(vmem_limit_bytes=32 * 1024 * 1024),
    )(q.reshape(2, 16, 2, 64, 128), jnp.asarray(np.ascontiguousarray(c["pi"].T)))
    return from_rows(lesser), from_rows(greater)


def solution(mesh):
    in_specs = (P("energy", None, "elem"), P("energy", None, "elem"), P("elem", None, None))
    out_specs = (P("energy", None, "elem"), P("energy", None, "elem"))
    return jax.shard_map(
        per_device, mesh=mesh, in_specs=in_specs, out_specs=out_specs, check_vma=False
    )
```

```python
import functools
import math

import jax
import jax.numpy as jnp
import ml_dtypes
import numpy as np
from jax import lax
from jax.experimental import pallas as pl
from jax.experimental.pallas import tpu as pltpu
from jax.sharding import PartitionSpec as P

NE = 2048
NT = 4096
MESH = pl.DeviceIdType.MESH
BF16 = ml_dtypes.bfloat16


def rotation(rows, cols, length, sign):
    theta = np.outer(rows, cols) % length * (2.0 * math.pi / length)
    cos, sin = np.cos(theta), sign * np.sin(theta)
    return np.stack([np.stack([cos, -sin], -1), np.stack([sin, cos], -1)], 1)


def widen(small):
    a, _, b, _ = small.shape
    full = np.einsum("acbd,rs->acrbds", small, np.eye(8))
    return full.reshape(a * 16, b * 16).astype(BF16)


@functools.cache
def constants():
    n = np.arange(64)
    half = np.arange(32)
    k1 = np.stack([widen(rotation(n, half, 64, s)) for s in (-1, 1)])
    a2 = []
    for s in (-1, 1):
        m = rotation(n, n, 64, s).transpose(1, 0, 2, 3).reshape(2, 64, 8, 8, 2)
        a2.append(m.transpose(0, 1, 2, 4, 3).reshape(128, 128))
    a2 = np.stack(a2).astype(BF16)
    b3 = []
    for s in (1, -1):
        m = rotation(n, n, 64, s).reshape(8, 8, 2, 64, 2)
        b3.append(m.transpose(0, 2, 1, 4, 3).reshape(128, 128))
    b3 = np.concatenate(b3).astype(BF16)
    k4 = []
    for s in (1, -1):
        m = rotation(half, n, 64, s)
        m = np.stack([m[:, 1], -m[:, 0]], 1)
        k4.append(widen(m))
    k4 = np.stack(k4)
    theta = np.outer(n, n) * (2.0 * math.pi / NT)
    tw = np.stack([np.cos(theta), np.sin(theta)])
    t1 = tw.reshape(2, 64, 2, 2, 2, 8).transpose(0, 2, 1, 5, 3, 4)
    t1 = np.repeat(t1.reshape(2, 2, 512, 4), 64, axis=3).astype(np.float32)
    t3 = tw / (NT * math.sqrt(NE))
    t3 = t3.reshape(2, 16, 4, 64).transpose(0, 1, 3, 2)
    t3 = np.repeat(t3, 64, axis=3).astype(np.float32)
    out_row = np.arange(256).reshape(8, 16, 2).transpose(1, 2, 0).reshape(-1)
    pi = np.zeros((256, 256))
    pi[np.arange(256), out_row] = 1.0
    return dict(k1=k1, a2=a2, b3=b3, k4=k4, t1=t1, t3=t3, pi=pi.astype(BF16))


def dot(a, b):
    return jnp.dot(a, b, preferred_element_type=jnp.float32)


def swap_halves(first, second):
    width = first.shape[-1]
    axis = first.ndim - 1
    low_parts, high_parts = [], []
    for start in range(0, width, 128):
        a = first[..., start : start + 128]
        b = second[..., start : start + 128]
        lane = lax.broadcasted_iota(jnp.int32, a.shape, axis)
        low_parts.append(jnp.where(lane < 64, a, pltpu.roll(b, 64, axis)))
        high_parts.append(jnp.where(lane < 64, pltpu.roll(a, 64, axis), b))
    if len(low_parts) == 1:
        return low_parts[0], high_parts[0]
    return jnp.concatenate(low_parts, axis), jnp.concatenate(high_parts, axis)


def main_kernel(
    n,
    vl, vg, part, pi_h, k1_h, a2_h, b3_h, k4_h, t1_h, t3_h,
    q_ref,
    x_in, send, recv, zz, bb, outs,
    pi, k1, a2, b3, k4, t1, t3,
    in_sem, const_sem, send_sem, recv_sem, back_send_sem, back_recv_sem,
):
    e = lax.axis_index("energy")
    l = lax.axis_index("elem")
    other = l + 1 - 2 * lax.rem(l, 2)
    barrier = pltpu.get_barrier_semaphore()

    loads = [
        pltpu.make_async_copy(pi_h, pi, const_sem.at[0]),
        pltpu.make_async_copy(vl, x_in.at[0], in_sem.at[0]),
        pltpu.make_async_copy(vg, x_in.at[1], in_sem.at[1]),
    ]
    for copy in loads:
        copy.start()

    def greet(i, carry):
        dst = lax.rem(e + i, n)
        pl.semaphore_signal(barrier, inc=1, device_id=(dst, l), device_id_type=MESH)
        return carry

    def greet_other(i, carry):
        dst = lax.rem(e + i, n)
        pl.semaphore_signal(barrier, inc=1, device_id=(dst, other), device_id_type=MESH)
        return carry

    lax.fori_loop(1, n, greet, 0)
    lax.fori_loop(0, n, greet_other, 0)

    consts = [
        pltpu.make_async_copy(src, dst, const_sem.at[i + 1])
        for i, (src, dst) in enumerate(
            ((k1_h, k1), (t1_h, t1), (a2_h, a2), (b3_h, b3), (t3_h, t3), (k4_h, k4))
        )
    ]
    for copy in consts:
        copy.start()

    def pack(arr):
        for gh in range(4):
            base = gh * 512
            rhs = jnp.concatenate(
                [x_in[arr, base : base + 256, :], x_in[arr, base + 256 : base + 512, :]], axis=1
            )
            rows = dot(pi[...], rhs)
            even, odd = swap_halves(rows[:, :128], rows[:, 128:])
            at = slice(gh * 16, gh * 16 + 16)
            send[arr, :, 0, at, :] = even.reshape(16, 16, 128).astype(jnp.bfloat16)
            send[arr, :, 1, at, :] = odd.reshape(16, 16, 128).astype(jnp.bfloat16)

    def out_copy(arr, dst, elem):
        return pltpu.make_async_remote_copy(
            src_ref=send.at[arr, lax.div(dst, 2), lax.rem(dst, 2)],
            dst_ref=recv.at[arr, e],
            send_sem=send_sem.at[arr],
            recv_sem=recv_sem.at[arr],
            device_id=(dst, elem),
            device_id_type=MESH,
        )

    loads[0].wait()
    loads[1].wait()
    pack(0)
    pl.semaphore_wait(barrier, 2 * n - 1)

    def send_lesser(i, carry):
        out_copy(0, lax.rem(e + i, n), l).start()
        return carry

    def send_greater(i, carry):
        out_copy(1, lax.rem(e + i, n), other).start()
        return carry

    lax.fori_loop(1, n, send_lesser, 0)
    pltpu.make_async_copy(
        send.at[0, lax.div(e, 2), lax.rem(e, 2)], recv.at[0, e], recv_sem.at[0]
    ).start()
    loads[2].wait()
    pack(1)
    lax.fori_loop(0, n, send_greater, 0)

    row = part[pl.ds(e, 1), :] & 63
    row = jnp.concatenate([row, row + 64], axis=1)
    one_hot = jnp.where(lax.broadcasted_iota(jnp.int32, (128, 128), 0) == row, 1.0, 0.0)
    one_hot = one_hot.astype(jnp.bfloat16)

    consts[0].wait()
    consts[1].wait()

    for arr in range(2):
        pltpu.make_async_copy(recv.at[arr], recv.at[arr], recv_sem.at[arr]).wait()
        sign = 1.0 if arr == 0 else -1.0
        for gp in range(2):
            sides = []
            for gh in (2 * gp, 2 * gp + 1):
                side = recv[arr, :, gh * 16 : gh * 16 + 16, :].reshape(512, 128)
                if arr == 1:
                    side = dot(side, one_hot).astype(jnp.bfloat16)
                sides.append(side)
            rhs = jnp.concatenate(sides, axis=1)
            for m in range(4):
                y = dot(k1[arr, m * 256 : (m + 1) * 256, :], rhs).reshape(16, 2, 8, 256)
                y_re, y_im = y[:, 0], y[:, 1]
                cos = t1[0, gp, m * 128 : (m + 1) * 128, :].reshape(16, 8, 256)
                sin = t1[1, gp, m * 128 : (m + 1) * 128, :].reshape(16, 8, 256) * sign
                z_re = cos * y_re + sin * y_im
                z_im = cos * y_im - sin * y_re
                z = jnp.stack([z_re, z_im], axis=1).reshape(8, 2, 16, 256)
                low, high = swap_halves(z[:, 0], z[:, 1])
                low, high = low.astype(jnp.bfloat16), high.astype(jnp.bfloat16)
                for side in range(2):
                    lanes = slice(side * 128, side * 128 + 128)
                    g = 4 * gp + 2 * side
                    zz[arr, m * 8 : m * 8 + 8, g * 16 : g * 16 + 16, :] = low[..., lanes]
                    zz[arr, m * 8 : m * 8 + 8, g * 16 + 16 : g * 16 + 32, :] = high[..., lanes]

    for copy in consts[2:5]:
        copy.wait()

    def middle(j, carry):
        def spectrum(arr):
            rhs = jnp.concatenate([zz[arr, 2 * j], zz[arr, 2 * j + 1]], axis=1)
            return dot(a2[arr], rhs)

        one, two = spectrum(0), spectrum(1)
        l_re, l_im, g_re, g_im = one[:64], one[64:], two[:64], two[64:]
        prod = jnp.concatenate([l_re * g_re - l_im * g_im, l_re * g_im + l_im * g_re], axis=0)
        a = dot(b3[...], prod.astype(jnp.bfloat16)).reshape(2, 8, 2, 8, 256)
        cos = t3[0, j].reshape(8, 8, 256)
        sin = t3[1, j].reshape(8, 8, 256)
        for path, s in ((0, sin), (1, -sin)):
            a_re, a_im = a[path, :, 0], a[path, :, 1]
            b_re = cos * a_re - s * a_im
            b_im = cos * a_im + s * a_re
            b = jnp.stack([b_re, b_im], axis=1).reshape(4, 2, 16, 256)
            low, high = swap_halves(b[:, 0], b[:, 1])
            low, high = low.astype(jnp.bfloat16), high.astype(jnp.bfloat16)
            for side in range(2):
                lanes = slice(side * 128, side * 128 + 128)
                k2 = 4 * j + 2 * side
                bb[path, :, k2, :, :] = low[..., lanes]
                bb[path, :, k2 + 1, :, :] = high[..., lanes]
        return carry

    lax.fori_loop(0, 16, middle, 0, unroll=8)
    consts[5].wait()

    def back_copy(path, dst, elem):
        return pltpu.make_async_remote_copy(
            src_ref=outs.at[path, dst],
            dst_ref=q_ref.at[path, e],
            send_sem=back_send_sem.at[path],
            recv_sem=back_recv_sem.at[path],
            device_id=(dst, elem),
            device_id_type=MESH,
        )

    def back_lesser(i, carry):
        back_copy(0, lax.rem(e + i, n), l).start()
        return carry

    def back_greater(i, carry):
        back_copy(1, lax.rem(e + i, n), other).start()
        return carry

    for path in range(2):
        for gp in range(2):
            rhs = jnp.concatenate(
                [bb[path, 2 * gp].reshape(1024, 128), bb[path, 2 * gp + 1].reshape(1024, 128)],
                axis=1,
            )
            for m in range(2):
                x = dot(k4[path, m * 256 : (m + 1) * 256, :], rhs).astype(jnp.bfloat16)
                for side in range(2):
                    part_x = x[:, side * 128 : side * 128 + 128]
                    if path == 1:
                        part_x = lax.dot_general(
                            part_x, one_hot, (((1,), (1,)), ((), ())), preferred_element_type=jnp.float32
                        ).astype(jnp.bfloat16)
                    gh = 2 * gp + side
                    outs[path, m * 16 : m * 16 + 16, gh * 16 : gh * 16 + 16, :] = part_x.reshape(
                        16, 16, 128
                    )
        if path == 0:
            lax.fori_loop(1, n, back_lesser, 0)
            pltpu.make_async_copy(outs.at[0, e], q_ref.at[0, e], back_recv_sem.at[0]).start()
        else:
            lax.fori_loop(0, n, back_greater, 0)

    for path in range(2):
        pltpu.make_async_copy(q_ref.at[path], q_ref.at[path], back_recv_sem.at[path]).wait()
    for arr in range(2):
        count = n - 1 + arr
        sent = outs.at[arr, pl.ds(0, count)]
        pltpu.make_async_copy(sent, sent, send_sem.at[arr]).wait()
        pltpu.make_async_copy(sent, sent, back_send_sem.at[arr]).wait()


def post_kernel(q, pi_t, lesser, greater):
    for path, out in ((0, lesser), (1, greater)):
        for gh in range(4):
            at = slice(gh * 16, gh * 16 + 16)
            even = q[path, :, 0, at, :].reshape(256, 128)
            odd = q[path, :, 1, at, :].reshape(256, 128)
            rows = dot(pi_t[...], jnp.concatenate([even, odd], axis=1))
            first, second = swap_halves(rows[:, :128], rows[:, 128:])
            out[gh * 512 : gh * 512 + 256, :] = first
            out[gh * 512 + 256 : gh * 512 + 512, :] = second


def as_rows(g):
    return g.reshape(64, 2, 16, 128).transpose(0, 2, 1, 3).reshape(2048, 128)


def from_rows(v):
    return v.reshape(64, 16, 2, 128).transpose(0, 2, 1, 3).reshape(64, 2, 2048)


def per_device(g_lesser, g_greater, partner):
    n = lax.axis_size("energy")
    c = constants()
    hbm = pl.BlockSpec(memory_space=pltpu.HBM)
    vmem = pl.BlockSpec(memory_space=pltpu.VMEM)
    names = ("pi", "k1", "a2", "b3", "k4", "t1", "t3")
    tables = [jnp.asarray(c[name]) for name in names]
    scratch = [
        pltpu.VMEM((2, 2048, 128), jnp.bfloat16),
        pltpu.VMEM((2, 16, 2, 64, 128), jnp.bfloat16),
        pltpu.VMEM((2, 32, 64, 128), jnp.bfloat16),
        pltpu.VMEM((2, 32, 128, 128), jnp.bfloat16),
        pltpu.VMEM((2, 4, 64, 16, 128), jnp.bfloat16),
        pltpu.VMEM((2, 32, 64, 128), jnp.bfloat16),
    ]
    scratch += [pltpu.VMEM(t.shape, t.dtype) for t in tables]
    scratch += [
        pltpu.SemaphoreType.DMA((2,)),
        pltpu.SemaphoreType.DMA((7,)),
        pltpu.SemaphoreType.DMA((2,)),
        pltpu.SemaphoreType.DMA((2,)),
        pltpu.SemaphoreType.DMA((2,)),
        pltpu.SemaphoreType.DMA((2,)),
    ]
    q = pl.pallas_call(
        functools.partial(main_kernel, n),
        out_shape=jax.ShapeDtypeStruct((2, 32, 64, 128), jnp.bfloat16),
        in_specs=[hbm, hbm, vmem] + [hbm] * 7,
        out_specs=hbm,
        scratch_shapes=scratch,
        compiler_params=pltpu.CompilerParams(
            collective_id=0, has_side_effects=True, vmem_limit_bytes=64 * 1024 * 1024
        ),
    )(as_rows(g_lesser), as_rows(g_greater), partner[0], *tables)
    lesser, greater = pl.pallas_call(
        post_kernel,
        out_shape=[jax.ShapeDtypeStruct((2048, 128), jnp.float32)] * 2,
        in_specs=[vmem, vmem],
        out_specs=[vmem, vmem],
        compiler_params=pltpu.CompilerParams(vmem_limit_bytes=64 * 1024 * 1024),
    )(q.reshape(2, 16, 2, 64, 128), jnp.asarray(np.ascontiguousarray(c["pi"].T)))
    return from_rows(lesser), from_rows(greater)


def solution(mesh):
    in_specs = (P("energy", None, "elem"), P("energy", None, "elem"), P("elem", None, None))
    out_specs = (P("energy", None, "elem"), P("energy", None, "elem"))
    return jax.shard_map(
        per_device, mesh=mesh, in_specs=in_specs, out_specs=out_specs, check_vma=False
    )
```

```python
import functools
import math

import jax
import jax.numpy as jnp
import ml_dtypes
import numpy as np
from jax import lax
from jax.experimental import pallas as pl
from jax.experimental.pallas import tpu as pltpu
from jax.sharding import PartitionSpec as P

NE = 2048
NT = 4096
MESH = pl.DeviceIdType.MESH
BF16 = ml_dtypes.bfloat16


def rotation(rows, cols, length, sign):
    theta = np.outer(rows, cols) % length * (2.0 * math.pi / length)
    cos, sin = np.cos(theta), sign * np.sin(theta)
    return np.stack([np.stack([cos, -sin], -1), np.stack([sin, cos], -1)], 1)


def widen(small):
    a, _, b, _ = small.shape
    full = np.einsum("acbd,rs->acrbds", small, np.eye(8))
    return full.reshape(a * 16, b * 16).astype(BF16)


@functools.cache
def constants():
    n = np.arange(64)
    half = np.arange(32)
    k1 = np.stack([widen(rotation(n, half, 64, s)) for s in (-1, 1)])
    a2 = []
    for s in (-1, 1):
        m = rotation(n, n, 64, s).transpose(1, 0, 2, 3).reshape(2, 64, 8, 8, 2)
        a2.append(m.transpose(0, 1, 2, 4, 3).reshape(128, 128))
    a2 = np.stack(a2).astype(BF16)
    b3 = []
    for s in (1, -1):
        m = rotation(n, n, 64, s).reshape(8, 8, 2, 64, 2)
        b3.append(m.transpose(0, 2, 1, 4, 3).reshape(128, 128))
    b3 = np.concatenate(b3).astype(BF16)
    k4 = []
    for s in (1, -1):
        m = rotation(half, n, 64, s)
        m = np.stack([m[:, 1], -m[:, 0]], 1)
        k4.append(widen(m))
    k4 = np.stack(k4)
    theta = np.outer(n, n) * (2.0 * math.pi / NT)
    tw = np.stack([np.cos(theta), np.sin(theta)])
    t1 = tw.reshape(2, 64, 8, 8).transpose(0, 1, 3, 2)
    t1 = np.repeat(t1.reshape(2, 512, 8), 32, axis=2).astype(np.float32)
    t3 = tw / (NT * math.sqrt(NE))
    t3 = t3.reshape(2, 8, 8, 64).transpose(0, 1, 3, 2)
    t3 = np.repeat(t3, 32, axis=3).astype(np.float32)
    out_row = np.arange(256).reshape(8, 16, 2).transpose(1, 2, 0).reshape(-1)
    pi = np.zeros((256, 256))
    pi[np.arange(256), out_row] = 1.0
    return dict(k1=k1, a2=a2, b3=b3, k4=k4, t1=t1, t3=t3, pi=pi.astype(BF16))


def dot(a, b):
    return jnp.dot(a, b, preferred_element_type=jnp.float32)


def swap(a, b, width):
    axis = a.ndim - 1
    even = (lax.broadcasted_iota(jnp.int32, a.shape, axis) & width) == 0
    first = jnp.where(even, a, pltpu.roll(b, width, axis))
    second = jnp.where(even, pltpu.roll(a, 128 - width, axis), b)
    return first, second


def quarters(tiles):
    p0, p2 = swap(tiles[0], tiles[2], 64)
    p1, p3 = swap(tiles[1], tiles[3], 64)
    return (*swap(p0, p1, 32), *swap(p2, p3, 32))


def main_kernel(
    n,
    vl, vg, part, pi_h, k1_h, a2_h, b3_h, k4_h, t1_h, t3_h,
    q_l, q_g,
    x_in, send_g, send_l, recv_g, recv_l, zz, bb, outs_g, outs_l,
    pi, k1, a2, b3, k4, t1, t3,
    in_sem, const_sem, send_sem, recv_sem, back_send_sem, back_recv_sem,
):
    e = lax.axis_index("energy")
    l = lax.axis_index("elem")
    other = l + 1 - 2 * lax.rem(l, 2)
    barrier = pltpu.get_barrier_semaphore()

    loads = [
        pltpu.make_async_copy(pi_h, pi, const_sem.at[0]),
        pltpu.make_async_copy(vg, x_in.at[1], in_sem.at[1]),
        pltpu.make_async_copy(vl, x_in.at[0], in_sem.at[0]),
    ]
    for copy in loads:
        copy.start()

    def greet(i, carry):
        dst = lax.rem(e + i, n)
        pl.semaphore_signal(barrier, inc=1, device_id=(dst, l), device_id_type=MESH)
        return carry

    def greet_other(i, carry):
        dst = lax.rem(e + i, n)
        pl.semaphore_signal(barrier, inc=1, device_id=(dst, other), device_id_type=MESH)
        return carry

    lax.fori_loop(0, n, greet_other, 0)
    lax.fori_loop(1, n, greet, 0)

    consts = [
        pltpu.make_async_copy(src, dst, const_sem.at[i + 1])
        for i, (src, dst) in enumerate(
            ((k1_h, k1), (t1_h, t1), (a2_h, a2), (b3_h, b3), (t3_h, t3), (k4_h, k4))
        )
    ]
    for copy in consts:
        copy.start()

    def sorted_rows(arr, gh):
        base = gh * 512
        rhs = jnp.concatenate(
            [x_in[arr, base : base + 256, :], x_in[arr, base + 256 : base + 512, :]], axis=1
        )
        rows = dot(pi[...], rhs).astype(jnp.bfloat16)
        return rows[:, :128], rows[:, 128:]

    loads[0].wait()
    loads[1].wait()
    for gh in range(4):
        sides = swap(*sorted_rows(1, gh), 64)
        for e_lo in range(2):
            send_g[:, e_lo, gh * 16 : gh * 16 + 16, :] = sides[e_lo].reshape(16, 16, 128)

    def put_greater(i, carry):
        dst = lax.rem(e + i, n)
        pltpu.make_async_remote_copy(
            src_ref=send_g.at[lax.div(dst, 2), lax.rem(dst, 2)],
            dst_ref=recv_g.at[e],
            send_sem=send_sem.at[2],
            recv_sem=recv_sem.at[2],
            device_id=(dst, other),
            device_id_type=MESH,
        ).start()
        return carry

    pl.semaphore_wait(barrier, 2 * n - 1)
    lax.fori_loop(0, n, put_greater, 0)

    loads[2].wait()
    for g_hi in range(2):
        tiles = quarters((*sorted_rows(0, 2 * g_hi), *sorted_rows(0, 2 * g_hi + 1)))
        at = slice(g_hi * 16, g_hi * 16 + 16)
        for e_lo in range(2):
            for h in range(2):
                send_l[h, :, e_lo, at, :] = tiles[2 * e_lo + h].reshape(16, 16, 128)

    for h in range(2):

        def put_lesser(i, carry):
            dst = lax.rem(e + i, n)
            pltpu.make_async_remote_copy(
                src_ref=send_l.at[h, lax.div(dst, 2), lax.rem(dst, 2)],
                dst_ref=recv_l.at[h, e],
                send_sem=send_sem.at[h],
                recv_sem=recv_sem.at[h],
                device_id=(dst, l),
                device_id_type=MESH,
            ).start()
            return carry

        pltpu.make_async_copy(
            send_l.at[h, lax.div(e, 2), lax.rem(e, 2)], recv_l.at[h, e], recv_sem.at[h]
        ).start()
        lax.fori_loop(1, n, put_lesser, 0)

    row = part[pl.ds(e, 1), :] & 63
    row = jnp.concatenate([row, row], axis=1)
    first, second = swap(row, row, 32)
    lane = lax.broadcasted_iota(jnp.int32, (1, 128), 1)
    shift = (lane >> 5) * 64
    target = jnp.concatenate([first + shift, second + shift], axis=1)
    one_hot = jnp.where(lax.broadcasted_iota(jnp.int32, (256, 256), 0) == target, 1.0, 0.0)
    one_hot = one_hot.astype(jnp.bfloat16)

    def outer_stage(arr, h, rhs):
        sign = 1.0 if arr == 0 else -1.0
        for m in range(4):
            y = dot(k1[arr, m * 256 : (m + 1) * 256, :], rhs).reshape(16, 2, 8, 256)
            y_re, y_im = y[:, 0], y[:, 1]
            cos = t1[0, m * 128 : (m + 1) * 128, :].reshape(16, 8, 256)
            sin = t1[1, m * 128 : (m + 1) * 128, :].reshape(16, 8, 256) * sign
            z_re = cos * y_re + sin * y_im
            z_im = cos * y_im - sin * y_re
            z = jnp.stack([z_re, z_im], axis=1).reshape(4, 4, 16, 256).astype(jnp.bfloat16)
            for g_hi in range(2):
                tiles = quarters([z[:, i, :, g_hi * 128 : g_hi * 128 + 128] for i in range(4)])
                for g4 in range(4):
                    g = 4 * g_hi + g4
                    zz[arr, h, m * 4 : m * 4 + 4, g * 16 : g * 16 + 16, :] = tiles[g4]

    def middle_stage(h):
        def body(j, carry):
            def spectrum(arr):
                rhs = jnp.concatenate([zz[arr, h, 2 * j], zz[arr, h, 2 * j + 1]], axis=1)
                return dot(a2[arr], rhs)

            one, two = spectrum(0), spectrum(1)
            l_re, l_im, g_re, g_im = one[:64], one[64:], two[:64], two[64:]
            prod = jnp.concatenate([l_re * g_re - l_im * g_im, l_re * g_im + l_im * g_re], axis=0)
            a = dot(b3[...], prod.astype(jnp.bfloat16)).reshape(2, 8, 2, 8, 256)
            cos = t3[0, j].reshape(8, 8, 256)
            sin = t3[1, j].reshape(8, 8, 256)
            for path, s in ((0, sin), (1, -sin)):
                a_re, a_im = a[path, :, 0], a[path, :, 1]
                b_re = cos * a_re - s * a_im
                b_im = cos * a_im + s * a_re
                b = jnp.stack([b_re, b_im], axis=1).reshape(2, 4, 16, 256).astype(jnp.bfloat16)
                for side in range(2):
                    tiles = quarters([b[:, i, :, side * 128 : side * 128 + 128] for i in range(4)])
                    for low in range(4):
                        bb[path, h, :, 8 * j + 4 * side + low, :, :] = tiles[low]
            return carry

        lax.fori_loop(0, 8, body, 0, unroll=8)

    def last_stage(path, h, m):
        rhs = jnp.concatenate(
            [bb[path, h, 0].reshape(1024, 128), bb[path, h, 1].reshape(1024, 128)], axis=1
        )
        return dot(k4[path, m * 256 : (m + 1) * 256, :], rhs).astype(jnp.bfloat16)

    consts[0].wait()
    consts[1].wait()
    pltpu.make_async_copy(recv_g, recv_g, recv_sem.at[2]).wait()
    moved = []
    for g_hi in range(2):
        sides = [
            recv_g[:, gh * 16 : gh * 16 + 16, :].reshape(512, 128)
            for gh in (2 * g_hi, 2 * g_hi + 1)
        ]
        moved.append(dot(jnp.concatenate(sides, axis=1), one_hot).astype(jnp.bfloat16))
    for h in range(2):
        lanes = slice(h * 128, h * 128 + 128)
        outer_stage(1, h, jnp.concatenate([moved[0][:, lanes], moved[1][:, lanes]], axis=1))

    for copy in consts[2:]:
        copy.wait()

    for h in range(2):
        pltpu.make_async_copy(recv_l.at[h], recv_l.at[h], recv_sem.at[h]).wait()
        sides = [
            recv_l[h, :, g_hi * 16 : g_hi * 16 + 16, :].reshape(512, 128) for g_hi in range(2)
        ]
        outer_stage(0, h, jnp.concatenate(sides, axis=1))
        middle_stage(h)
        for m in range(2):
            x = last_stage(0, h, m)
            for g_hi in range(2):
                outs_l[h, m * 16 : m * 16 + 16, g_hi * 16 : g_hi * 16 + 16, :] = x[
                    :, g_hi * 128 : g_hi * 128 + 128
                ].reshape(16, 16, 128)

        def back_lesser(i, carry):
            dst = lax.rem(e + i, n)
            pltpu.make_async_remote_copy(
                src_ref=outs_l.at[h, dst],
                dst_ref=q_l.at[h, e],
                send_sem=back_send_sem.at[h],
                recv_sem=back_recv_sem.at[h],
                device_id=(dst, l),
                device_id_type=MESH,
            ).start()
            return carry

        lax.fori_loop(1, n, back_lesser, 0)
        pltpu.make_async_copy(outs_l.at[h, e], q_l.at[h, e], back_recv_sem.at[h]).start()

    for m in range(2):
        xs = [last_stage(1, h, m) for h in range(2)]
        for g_hi in range(2):
            lanes = slice(g_hi * 128, g_hi * 128 + 128)
            x = lax.dot_general(
                jnp.concatenate([xs[0][:, lanes], xs[1][:, lanes]], axis=1),
                one_hot,
                (((1,), (1,)), ((), ())),
                preferred_element_type=jnp.float32,
            ).astype(jnp.bfloat16)
            for t in range(2):
                gh = 2 * g_hi + t
                outs_g[m * 16 : m * 16 + 16, gh * 16 : gh * 16 + 16, :] = x[
                    :, t * 128 : t * 128 + 128
                ].reshape(16, 16, 128)

    def back_greater(i, carry):
        dst = lax.rem(e + i, n)
        pltpu.make_async_remote_copy(
            src_ref=outs_g.at[dst],
            dst_ref=q_g.at[e],
            send_sem=back_send_sem.at[2],
            recv_sem=back_recv_sem.at[2],
            device_id=(dst, other),
            device_id_type=MESH,
        ).start()
        return carry

    lax.fori_loop(0, n, back_greater, 0)

    for h in range(2):
        pltpu.make_async_copy(q_l.at[h], q_l.at[h], back_recv_sem.at[h]).wait()
        sent = outs_l.at[h, pl.ds(0, n - 1)]
        pltpu.make_async_copy(sent, sent, send_sem.at[h]).wait()
        pltpu.make_async_copy(sent, sent, back_send_sem.at[h]).wait()
    pltpu.make_async_copy(outs_g, outs_g, send_sem.at[2]).wait()
    pltpu.make_async_copy(outs_g, outs_g, back_send_sem.at[2]).wait()
    pltpu.make_async_copy(q_g, q_g, back_recv_sem.at[2]).wait()


def post_kernel(q_l, q_g, pi_h, lesser, greater, in_l, in_g, pi, rows, in_sem, out_sem):
    loads = [
        pltpu.make_async_copy(src, dst, in_sem.at[i])
        for i, (src, dst) in enumerate(((pi_h, pi), (q_l, in_l), (q_g, in_g)))
    ]
    for copy in loads:
        copy.start()
    loads[0].wait()
    stores = []

    def place(path, gh, tiles):
        both = dot(pi[...], jnp.concatenate(tiles, axis=1))
        rows[path, gh, :256, :] = both[:, :128]
        rows[path, gh, 256:, :] = both[:, 128:]
        out = (lesser, greater)[path]
        stores.append(
            pltpu.make_async_copy(
                rows.at[path, gh], out.at[pl.ds(gh * 512, 512)], out_sem.at[path, gh]
            )
        )
        stores[-1].start()

    loads[1].wait()
    for g_hi in range(2):
        at = slice(g_hi * 16, g_hi * 16 + 16)
        tiles = quarters(
            [in_l[h, :, e_lo, at, :].reshape(256, 128) for e_lo in range(2) for h in range(2)]
        )
        place(0, 2 * g_hi, tiles[:2])
        place(0, 2 * g_hi + 1, tiles[2:])
    loads[2].wait()
    for gh in range(4):
        at = slice(gh * 16, gh * 16 + 16)
        place(1, gh, swap(*[in_g[:, e_lo, at, :].reshape(256, 128) for e_lo in range(2)], 64))
    for copy in stores:
        copy.wait()


def as_rows(g):
    return g.reshape(64, 2, 16, 128).transpose(0, 2, 1, 3).reshape(2048, 128)


def from_rows(v):
    return v.reshape(64, 16, 2, 128).transpose(0, 2, 1, 3).reshape(64, 2, 2048)


def per_device(g_lesser, g_greater, partner):
    n = lax.axis_size("energy")
    c = constants()
    hbm = pl.BlockSpec(memory_space=pltpu.HBM)
    vmem = pl.BlockSpec(memory_space=pltpu.VMEM)
    names = ("pi", "k1", "a2", "b3", "k4", "t1", "t3")
    tables = [jnp.asarray(c[name]) for name in names]
    bf16 = jnp.bfloat16
    scratch = [
        pltpu.VMEM((2, 2048, 128), bf16),
        pltpu.VMEM((16, 2, 64, 128), bf16),
        pltpu.VMEM((2, 16, 2, 32, 128), bf16),
        pltpu.VMEM((32, 64, 128), bf16),
        pltpu.VMEM((2, 32, 32, 128), bf16),
        pltpu.VMEM((2, 2, 16, 128, 128), bf16),
        pltpu.VMEM((2, 2, 2, 64, 16, 128), bf16),
        pltpu.VMEM((32, 64, 128), bf16),
        pltpu.VMEM((2, 32, 32, 128), bf16),
    ]
    scratch += [pltpu.VMEM(t.shape, t.dtype) for t in tables]
    scratch += [pltpu.SemaphoreType.DMA((k,)) for k in (2, 7, 3, 3, 3, 3)]
    q_l, q_g = pl.pallas_call(
        functools.partial(main_kernel, n),
        out_shape=[
            jax.ShapeDtypeStruct((2, 32, 32, 128), bf16),
            jax.ShapeDtypeStruct((32, 64, 128), bf16),
        ],
        in_specs=[hbm, hbm, vmem] + [hbm] * 7,
        out_specs=[hbm, hbm],
        scratch_shapes=scratch,
        compiler_params=pltpu.CompilerParams(
            collective_id=0, has_side_effects=True, vmem_limit_bytes=64 * 1024 * 1024
        ),
    )(as_rows(g_lesser), as_rows(g_greater), partner[0], *tables)
    pi_t = jnp.asarray(np.ascontiguousarray(c["pi"].T))
    lesser, greater = pl.pallas_call(
        post_kernel,
        out_shape=[jax.ShapeDtypeStruct((2048, 128), jnp.float32)] * 2,
        in_specs=[hbm] * 3,
        out_specs=[hbm] * 2,
        scratch_shapes=[
            pltpu.VMEM((2, 16, 2, 32, 128), bf16),
            pltpu.VMEM((16, 2, 64, 128), bf16),
            pltpu.VMEM((256, 256), bf16),
            pltpu.VMEM((2, 4, 512, 128), jnp.float32),
            pltpu.SemaphoreType.DMA((3,)),
            pltpu.SemaphoreType.DMA((2, 4)),
        ],
        compiler_params=pltpu.CompilerParams(vmem_limit_bytes=64 * 1024 * 1024),
    )(q_l.reshape(2, 16, 2, 32, 128), q_g.reshape(16, 2, 64, 128), pi_t)
    return from_rows(lesser), from_rows(greater)


def solution(mesh):
    in_specs = (P("energy", None, "elem"), P("energy", None, "elem"), P("elem", None, None))
    out_specs = (P("energy", None, "elem"), P("energy", None, "elem"))
    return jax.shard_map(
        per_device, mesh=mesh, in_specs=in_specs, out_specs=out_specs, check_vma=False
    )
```

```python
import functools
import math

import jax
import jax.numpy as jnp
import ml_dtypes
import numpy as np
from jax import lax
from jax.experimental import pallas as pl
from jax.experimental.pallas import tpu as pltpu
from jax.sharding import PartitionSpec as P

NE = 2048
NT = 4096
MESH = pl.DeviceIdType.MESH
BF16 = ml_dtypes.bfloat16
MAIN_VMEM = 64 * 1024 * 1024
POST_VMEM = 64 * 1024 * 1024


def rotation(rows, cols, length, sign):
    theta = np.outer(rows, cols) % length * (2.0 * math.pi / length)
    cos, sin = np.cos(theta), sign * np.sin(theta)
    return np.stack([np.stack([cos, -sin], -1), np.stack([sin, cos], -1)], 1)


def widen(small):
    a, _, b, _ = small.shape
    full = np.einsum("acbd,rs->acrbds", small, np.eye(8))
    return full.reshape(a * 16, b * 16).astype(BF16)


@functools.cache
def constants():
    n = np.arange(64)
    half = np.arange(32)
    k1 = np.stack([widen(rotation(n, half, 64, s)) for s in (-1, 1)])
    a2 = []
    for s in (-1, 1):
        m = rotation(n, n, 64, s).transpose(1, 0, 2, 3).reshape(2, 64, 8, 8, 2)
        a2.append(m.transpose(0, 1, 2, 4, 3).reshape(128, 128))
    a2 = np.stack(a2).astype(BF16)
    b3 = []
    for s in (1, -1):
        m = rotation(n, n, 64, s).reshape(8, 8, 2, 64, 2)
        b3.append(m.transpose(0, 2, 1, 4, 3).reshape(128, 128))
    b3 = np.concatenate(b3).astype(BF16)
    k4 = []
    for s in (1, -1):
        m = rotation(half, n, 64, s)
        m = np.stack([m[:, 1], -m[:, 0]], 1)
        k4.append(widen(m))
    k4 = np.stack(k4)
    theta = np.outer(n, n) * (2.0 * math.pi / NT)
    tw = np.stack([np.cos(theta), np.sin(theta)])
    t1 = tw.reshape(2, 64, 8, 8).transpose(0, 1, 3, 2)
    t1 = np.repeat(t1.reshape(2, 512, 8), 32, axis=2).astype(np.float32)
    t3 = tw / (NT * math.sqrt(NE))
    t3 = t3.reshape(2, 8, 8, 64).transpose(0, 1, 3, 2)
    t3 = np.repeat(t3, 32, axis=3).astype(np.float32)
    k4 = k4.reshape(2, 512, 2, 512).transpose(0, 2, 1, 3).reshape(2048, 512)
    small = np.concatenate([a2[0], a2[1], b3[:128], b3[128:]], axis=1)
    wide = np.concatenate([k1.reshape(2048, 512), k4, small])
    return wide, np.concatenate([t1.reshape(2, 512, 256), t3.reshape(2, 512, 256)])


def far_first():
    hops = (0, 1, 2, 1)
    return sorted(range(32), key=lambda i: -(hops[i >> 3] + hops[(i >> 1) & 3] + (i & 1)))


def dot(a, b):
    return jnp.dot(a, b, preferred_element_type=jnp.float32)


def swap(a, b, width):
    axis = a.ndim - 1
    even = (lax.broadcasted_iota(jnp.int32, a.shape, axis) & width) == 0
    first = jnp.where(even, a, pltpu.roll(b, width, axis))
    second = jnp.where(even, pltpu.roll(a, 128 - width, axis), b)
    return first, second


def quarters(tiles):
    p0, p2 = swap(tiles[0], tiles[2], 64)
    p1, p3 = swap(tiles[1], tiles[3], 64)
    return (*swap(p0, p1, 32), *swap(p2, p3, 32))


def sort_matrix(back):
    one = lax.broadcasted_iota(jnp.int32, (256, 256), 0)
    two = lax.broadcasted_iota(jnp.int32, (256, 256), 1)
    if back:
        one, two = two, one
    hit = ((one >> 3) == (two & 31)) & ((one & 7) == (two >> 5))
    return jnp.where(hit, 1.0, 0.0).astype(jnp.bfloat16)


def main_kernel(
    vl, vg, part_h, wide_h, tw_h,
    q_l, q_g,
    x_in, part, send_l, send_g, recv_l, recv_g, zz, bb, outs_l, outs_g, relay, wide, tw,
    in_sem, swap_sem, send_sem, recv_sem, back_send_sem, back_recv_sem, relay_send_sem, relay_recv_sem,
):
    e = lax.axis_index("energy")
    l = lax.axis_index("elem")
    sibling = (e, l + 1 - 2 * lax.rem(l, 2))
    order = far_first()
    n = len(order)
    barrier = pltpu.get_barrier_semaphore()

    load_l = pltpu.make_async_copy(vl, x_in.at[0], in_sem.at[0])
    load_part = pltpu.make_async_copy(part_h, part, in_sem.at[1])
    load_l.start()
    load_part.start()

    def greet(i, carry):
        pl.semaphore_signal(
            barrier, inc=1, device_id=(lax.rem(e + i, n), l), device_id_type=MESH
        )
        return carry

    pl.semaphore_signal(barrier, inc=1, device_id=sibling, device_id_type=MESH)
    lax.fori_loop(1, n, greet, 0)

    loads = [
        pltpu.make_async_copy(src, dst, in_sem.at[2 + i])
        for i, (src, dst) in enumerate(
            (
                (wide_h.at[pl.ds(0, 2048)], wide.at[pl.ds(0, 2048)]),
                (tw_h, tw),
                (wide_h.at[pl.ds(4096, 128)], wide.at[pl.ds(4096, 128)]),
                (wide_h.at[pl.ds(2048, 2048)], wide.at[pl.ds(2048, 2048)]),
            )
        )
    ]
    for copy in loads:
        copy.start()

    def scatter(source, target, send, recv):
        for i in order:
            dst = jnp.bitwise_xor(e, i)
            if i == 0:
                pltpu.make_async_copy(source(dst), target.at[e], recv).start()
            else:
                pltpu.make_async_remote_copy(
                    src_ref=source(dst),
                    dst_ref=target.at[e],
                    send_sem=send,
                    recv_sem=recv,
                    device_id=(dst, l),
                    device_id_type=MESH,
                ).start()

    def wait_bytes(ref, sem):
        pltpu.make_async_copy(ref, ref, sem).wait()

    pi = sort_matrix(False)

    def sorted_rows(arr, gh):
        base = gh * 512
        rhs = jnp.concatenate(
            [x_in[arr, base : base + 256, :], x_in[arr, base + 256 : base + 512, :]], axis=1
        )
        rows = dot(pi, rhs).astype(jnp.bfloat16)
        return rows[:, :128], rows[:, 128:]

    load_l.wait()
    for gh in range(4):
        sides = swap(*sorted_rows(0, gh), 64)
        for e_lo in range(2):
            send_l[:, e_lo, gh * 16 : gh * 16 + 16, :] = sides[e_lo].reshape(16, 16, 128)

    pl.semaphore_wait(barrier, n)
    trade = pltpu.make_async_remote_copy(
        src_ref=vg,
        dst_ref=x_in.at[1],
        send_sem=swap_sem.at[0],
        recv_sem=swap_sem.at[1],
        device_id=sibling,
        device_id_type=MESH,
    )
    trade.start()
    scatter(
        lambda d: send_l.at[lax.div(d, 2), lax.rem(d, 2)], recv_l, send_sem.at[2], recv_sem.at[2]
    )

    trade.wait()
    for g_hi in range(2):
        tiles = quarters((*sorted_rows(1, 2 * g_hi), *sorted_rows(1, 2 * g_hi + 1)))
        at = slice(g_hi * 16, g_hi * 16 + 16)
        for e_lo in range(2):
            for h in range(2):
                send_g[h, :, e_lo, at, :] = tiles[2 * e_lo + h].reshape(16, 16, 128)
    for h in range(2):
        scatter(
            lambda d: send_g.at[h, lax.div(d, 2), lax.rem(d, 2)],
            recv_g.at[h],
            send_sem.at[h],
            recv_sem.at[h],
        )

    load_part.wait()
    row = part[pl.ds(e, 1), :] & 63
    row = jnp.concatenate([row] * 4, axis=1)
    lane = lax.broadcasted_iota(jnp.int32, (1, 256), 1)
    target = (row >> 5) * 128 + (lane >> 6) * 32 + (row & 31)
    one_hot = jnp.where(lax.broadcasted_iota(jnp.int32, (256, 256), 0) == target, 1.0, 0.0)
    one_hot = one_hot.astype(jnp.bfloat16)

    def outer_stage(arr, h, rhs):
        sign = 1.0 if arr == 0 else -1.0
        for m in range(4):
            base = arr * 1024 + m * 256
            y = dot(wide[base : base + 256, :], rhs).reshape(16, 2, 8, 256)
            y_re, y_im = y[:, 0], y[:, 1]
            cos = tw[0, m * 128 : (m + 1) * 128, :].reshape(16, 8, 256)
            sin = tw[1, m * 128 : (m + 1) * 128, :].reshape(16, 8, 256) * sign
            z_re = cos * y_re + sin * y_im
            z_im = cos * y_im - sin * y_re
            z = jnp.stack([z_re, z_im], axis=1).reshape(4, 4, 16, 256).astype(jnp.bfloat16)
            for g_hi in range(2):
                tiles = quarters([z[:, i, :, g_hi * 128 : g_hi * 128 + 128] for i in range(4)])
                for g4 in range(4):
                    g = 4 * g_hi + g4
                    zz[arr, h, m * 4 : m * 4 + 4, g * 16 : g * 16 + 16, :] = tiles[g4]

    def middle_stage(h):
        def body(j, carry):
            def spectrum(arr):
                rhs = jnp.concatenate([zz[arr, h, 2 * j], zz[arr, h, 2 * j + 1]], axis=1)
                return dot(wide[4096:4224, arr * 128 : arr * 128 + 128], rhs)

            one, two = spectrum(0), spectrum(1)
            l_re, l_im, g_re, g_im = one[:64], one[64:], two[:64], two[64:]
            prod = jnp.concatenate([l_re * g_re - l_im * g_im, l_re * g_im + l_im * g_re], axis=0)
            prod = prod.astype(jnp.bfloat16)
            at = pl.ds(pl.multiple_of(j * 64, 64), 64)
            cos = tw[2, at, :].reshape(8, 8, 256)
            sin = tw[3, at, :].reshape(8, 8, 256)
            for path, s in ((0, sin), (1, -sin)):
                b3 = wide[4096:4224, 256 + path * 128 : 384 + path * 128]
                a = dot(b3, prod).reshape(8, 2, 8, 256)
                a_re, a_im = a[:, 0], a[:, 1]
                b_re = cos * a_re - s * a_im
                b_im = cos * a_im + s * a_re
                b = jnp.stack([b_re, b_im], axis=1).reshape(2, 4, 16, 256).astype(jnp.bfloat16)
                for side in range(2):
                    tiles = quarters([b[:, i, :, side * 128 : side * 128 + 128] for i in range(4)])
                    for low in range(4):
                        bb[path, h, :, 8 * j + 4 * side + low, :, :] = tiles[low]
            return carry

        lax.fori_loop(0, 8, body, 0, unroll=8)

    def last_stage(path, h, m):
        rhs = jnp.concatenate(
            [bb[path, h, 0].reshape(1024, 128), bb[path, h, 1].reshape(1024, 128)], axis=1
        )
        base = 2048 + path * 1024 + m * 256
        k4 = jnp.concatenate(
            [wide[base : base + 256, :], wide[base + 512 : base + 768, :]], axis=1
        )
        return dot(k4, rhs).astype(jnp.bfloat16)

    loads[0].wait()
    loads[1].wait()
    wait_bytes(recv_l, recv_sem.at[2])
    moved = []
    for g_hi in range(2):
        sides = [
            recv_l[:, gh * 16 : gh * 16 + 16, :].reshape(512, 128)
            for gh in (2 * g_hi, 2 * g_hi + 1)
        ]
        moved.append(
            lax.dot_general(
                jnp.concatenate(sides, axis=1),
                one_hot,
                (((1,), (1,)), ((), ())),
                preferred_element_type=jnp.float32,
            ).astype(jnp.bfloat16)
        )
    for h in range(2):
        lanes = slice(h * 128, h * 128 + 128)
        outer_stage(0, h, jnp.concatenate([moved[0][:, lanes], moved[1][:, lanes]], axis=1))
    loads[2].wait()
    loads[3].wait()

    for h in range(2):
        wait_bytes(recv_g.at[h], recv_sem.at[h])
        sides = [
            recv_g[h, :, g_hi * 16 : g_hi * 16 + 16, :].reshape(512, 128) for g_hi in range(2)
        ]
        outer_stage(1, h, jnp.concatenate(sides, axis=1))
        middle_stage(h)
        for m in range(2):
            x = last_stage(1, h, m)
            for g_hi in range(2):
                outs_g[h, m * 16 : m * 16 + 16, g_hi * 16 : g_hi * 16 + 16, :] = x[
                    :, g_hi * 128 : g_hi * 128 + 128
                ].reshape(16, 16, 128)
        scatter(
            lambda d: outs_g.at[h, d], relay.at[h], back_send_sem.at[h], back_recv_sem.at[h]
        )

    for m in range(2):
        xs = [last_stage(0, h, m) for h in range(2)]
        for g_hi in range(2):
            lanes = slice(g_hi * 128, g_hi * 128 + 128)
            x = dot(jnp.concatenate([xs[0][:, lanes], xs[1][:, lanes]], axis=1), one_hot)
            x = x.astype(jnp.bfloat16)
            for t in range(2):
                gh = 2 * g_hi + t
                outs_l[m * 16 : m * 16 + 16, gh * 16 : gh * 16 + 16, :] = x[
                    :, t * 128 : t * 128 + 128
                ].reshape(16, 16, 128)
    scatter(lambda d: outs_l.at[d], q_l, back_send_sem.at[2], back_recv_sem.at[2])

    hands = []
    for h in range(2):
        wait_bytes(relay.at[h], back_recv_sem.at[h])
        hand = pltpu.make_async_remote_copy(
            src_ref=relay.at[h],
            dst_ref=q_g.at[h],
            send_sem=relay_send_sem.at[h],
            recv_sem=relay_recv_sem.at[h],
            device_id=sibling,
            device_id_type=MESH,
        )
        hand.start()
        hands.append(hand)
    for h in range(2):
        sent = outs_g.at[h, pl.ds(0, n - 1)]
        wait_bytes(sent, send_sem.at[h])
        wait_bytes(sent, back_send_sem.at[h])
    sent = outs_l.at[pl.ds(0, n - 1)]
    wait_bytes(sent, send_sem.at[2])
    wait_bytes(sent, back_send_sem.at[2])
    for hand in hands:
        hand.wait()
    wait_bytes(q_l, back_recv_sem.at[2])


def post_kernel(q_l, q_g, lesser, greater, in_l, in_g, rows, in_sem, out_sem):
    loads = [
        pltpu.make_async_copy(src, dst, in_sem.at[i])
        for i, (src, dst) in enumerate(((q_g, in_g), (q_l, in_l)))
    ]
    for copy in loads:
        copy.start()
    pi = sort_matrix(True)
    stores = []

    def place(path, gh, tiles):
        both = dot(pi, jnp.concatenate(tiles, axis=1))
        rows[path, gh, :256, :] = both[:, :128]
        rows[path, gh, 256:, :] = both[:, 128:]
        out = (lesser, greater)[path]
        stores.append(
            pltpu.make_async_copy(
                rows.at[path, gh], out.at[pl.ds(gh * 512, 512)], out_sem.at[path, gh]
            )
        )
        stores[-1].start()

    loads[0].wait()
    for g_hi in range(2):
        at = slice(g_hi * 16, g_hi * 16 + 16)
        tiles = quarters(
            [in_g[h, :, e_lo, at, :].reshape(256, 128) for e_lo in range(2) for h in range(2)]
        )
        place(1, 2 * g_hi, tiles[:2])
        place(1, 2 * g_hi + 1, tiles[2:])
    loads[1].wait()
    for gh in range(4):
        at = slice(gh * 16, gh * 16 + 16)
        place(0, gh, swap(*[in_l[:, e_lo, at, :].reshape(256, 128) for e_lo in range(2)], 64))
    for copy in stores:
        copy.wait()


def as_rows(g):
    return g.reshape(64, 2, 16, 128).transpose(0, 2, 1, 3).reshape(2048, 128)


def from_rows(v):
    return v.reshape(64, 16, 2, 128).transpose(0, 2, 1, 3).reshape(64, 2, 2048)


def per_device(g_lesser, g_greater, partner):
    tables = [jnp.asarray(table) for table in constants()]
    hbm = pl.BlockSpec(memory_space=pltpu.HBM)
    bf16 = jnp.bfloat16
    whole, chunks = (32, 64, 128), (2, 32, 32, 128)
    whole_lt, chunks_lt = (16, 2, 64, 128), (2, 16, 2, 32, 128)
    scratch = [
        pltpu.VMEM((2, 2048, 128), bf16),
        pltpu.VMEM((32, 64), jnp.int32),
        pltpu.VMEM(whole_lt, bf16),
        pltpu.VMEM(chunks_lt, bf16),
        pltpu.VMEM(whole, bf16),
        pltpu.VMEM(chunks, bf16),
        pltpu.VMEM((2, 2, 16, 128, 128), bf16),
        pltpu.VMEM((2, 2, 2, 64, 16, 128), bf16),
        pltpu.VMEM(whole, bf16),
        pltpu.VMEM(chunks, bf16),
        pltpu.VMEM(chunks, bf16),
    ]
    scratch += [pltpu.VMEM(t.shape, t.dtype) for t in tables]
    scratch += [pltpu.SemaphoreType.DMA((k,)) for k in (6, 2, 3, 3, 3, 3, 2, 2)]
    q_l, q_g = pl.pallas_call(
        main_kernel,
        out_shape=[jax.ShapeDtypeStruct(whole, bf16), jax.ShapeDtypeStruct(chunks, bf16)],
        in_specs=[hbm] * 5,
        out_specs=[hbm] * 2,
        scratch_shapes=scratch,
        compiler_params=pltpu.CompilerParams(
            collective_id=0, has_side_effects=True, vmem_limit_bytes=MAIN_VMEM
        ),
    )(as_rows(g_lesser), as_rows(g_greater), partner[0], *tables)
    lesser, greater = pl.pallas_call(
        post_kernel,
        out_shape=[jax.ShapeDtypeStruct((2048, 128), jnp.float32)] * 2,
        in_specs=[hbm] * 2,
        out_specs=[hbm] * 2,
        scratch_shapes=[
            pltpu.VMEM(whole_lt, bf16),
            pltpu.VMEM(chunks_lt, bf16),
            pltpu.VMEM((2, 4, 512, 128), jnp.float32),
            pltpu.SemaphoreType.DMA((2,)),
            pltpu.SemaphoreType.DMA((2, 4)),
        ],
        compiler_params=pltpu.CompilerParams(vmem_limit_bytes=POST_VMEM),
    )(q_l.reshape(whole_lt), q_g.reshape(chunks_lt))
    return from_rows(lesser), from_rows(greater)


def solution(mesh):
    in_specs = (P("energy", None, "elem"), P("energy", None, "elem"), P("elem", None, None))
    out_specs = (P("energy", None, "elem"), P("energy", None, "elem"))
    return jax.shard_map(
        per_device, mesh=mesh, in_specs=in_specs, out_specs=out_specs, check_vma=False
    )
```

```python
import functools
import math

import jax
import jax.numpy as jnp
import ml_dtypes
import numpy as np
from jax import lax
from jax.experimental import pallas as pl
from jax.experimental.pallas import tpu as pltpu
from jax.sharding import PartitionSpec as P

NE = 2048
NT = 4096
MESH = pl.DeviceIdType.MESH
BF16 = ml_dtypes.bfloat16
MAIN_VMEM = 60 * 1024 * 1024
POST_VMEM = 32 * 1024 * 1024


def rotation(rows, cols, length, sign):
    theta = np.outer(rows, cols) % length * (2.0 * math.pi / length)
    cos, sin = np.cos(theta), sign * np.sin(theta)
    return np.stack([np.stack([cos, -sin], -1), np.stack([sin, cos], -1)], 1)


def widen(small):
    a, _, b, _ = small.shape
    full = np.einsum("acbd,rs->acrbds", small, np.eye(8))
    return full.reshape(a * 16, b * 16).astype(BF16)


@functools.cache
def constants():
    n = np.arange(64)
    half = np.arange(32)
    k1 = np.stack([widen(rotation(n, half, 64, s)) for s in (-1, 1)])
    a2 = []
    for s in (-1, 1):
        m = rotation(n, n, 64, s).transpose(1, 0, 2, 3).reshape(2, 64, 8, 8, 2)
        a2.append(m.transpose(0, 1, 2, 4, 3).reshape(128, 128))
    a2 = np.stack(a2).astype(BF16)
    b3 = []
    for s in (1, -1):
        m = rotation(n, n, 64, s).reshape(8, 8, 2, 64, 2)
        b3.append(m.transpose(0, 2, 1, 4, 3).reshape(128, 128))
    b3 = np.concatenate(b3).astype(BF16)
    k4 = []
    for s in (1, -1):
        m = rotation(half, n, 64, s)
        m = np.stack([m[:, 1], -m[:, 0]], 1)
        k4.append(widen(m))
    k4 = np.stack(k4)
    theta = np.outer(n, n) * (2.0 * math.pi / NT)
    tw = np.stack([np.cos(theta), np.sin(theta)])
    t1 = tw.reshape(2, 64, 8, 8).transpose(0, 1, 3, 2)
    t1 = np.repeat(t1.reshape(2, 512, 8), 32, axis=2).astype(np.float32)
    t3 = tw / (NT * math.sqrt(NE))
    t3 = t3.reshape(2, 8, 8, 64).transpose(0, 1, 3, 2)
    t3 = np.repeat(t3, 32, axis=3).astype(np.float32)
    k4 = k4.reshape(2, 512, 2, 512).transpose(0, 2, 1, 3).reshape(2048, 512)
    small = np.concatenate([a2[0], a2[1], b3[:128], b3[128:]], axis=1)
    wide = np.concatenate([k1.reshape(2048, 512), k4, small])
    return wide, np.concatenate([t1.reshape(2, 512, 256), t3.reshape(2, 512, 256)])


def far_first():
    hops = (0, 1, 2, 1)
    return sorted(range(32), key=lambda i: -(hops[i >> 3] + hops[(i >> 1) & 3] + (i & 1)))


def dot(a, b):
    return jnp.dot(a, b, preferred_element_type=jnp.float32)


def swap(a, b, width):
    axis = a.ndim - 1
    even = (lax.broadcasted_iota(jnp.int32, a.shape, axis) & width) == 0
    first = jnp.where(even, a, pltpu.roll(b, width, axis))
    second = jnp.where(even, pltpu.roll(a, 128 - width, axis), b)
    return first, second


def quarters(tiles):
    p0, p2 = swap(tiles[0], tiles[2], 64)
    p1, p3 = swap(tiles[1], tiles[3], 64)
    return (*swap(p0, p1, 32), *swap(p2, p3, 32))


def sort_matrix(back):
    one = lax.broadcasted_iota(jnp.int32, (256, 256), 0)
    two = lax.broadcasted_iota(jnp.int32, (256, 256), 1)
    if back:
        one, two = two, one
    hit = ((one >> 3) == (two & 31)) & ((one & 7) == (two >> 5))
    return jnp.where(hit, 1.0, 0.0).astype(jnp.bfloat16)


def main_kernel(
    vl, vg, part_h, wide_h, tw_h,
    q,
    x_in, part, send_l, send_g, recv_l, recv_g, zz, bb, outs_l, outs_g, relay, wide, tw,
    in_sem, swap_sem, send_sem, recv_sem, back_send_sem, back_recv_sem, relay_send_sem, relay_recv_sem,
):
    e = lax.axis_index("energy")
    l = lax.axis_index("elem")
    sibling = (e, l + 1 - 2 * lax.rem(l, 2))
    order = far_first()
    n = len(order)
    barrier = pltpu.get_barrier_semaphore()

    load_l = pltpu.make_async_copy(vl, x_in.at[0], in_sem.at[0])
    load_part = pltpu.make_async_copy(part_h, part, in_sem.at[1])
    load_l.start()
    load_part.start()

    def greet(i, carry):
        pl.semaphore_signal(
            barrier, inc=1, device_id=(lax.rem(e + i, n), l), device_id_type=MESH
        )
        return carry

    pl.semaphore_signal(barrier, inc=1, device_id=sibling, device_id_type=MESH)
    lax.fori_loop(1, n, greet, 0)

    loads = [
        pltpu.make_async_copy(src, dst, in_sem.at[2 + i])
        for i, (src, dst) in enumerate(
            (
                (wide_h.at[pl.ds(0, 2048)], wide.at[pl.ds(0, 2048)]),
                (tw_h, tw),
                (wide_h.at[pl.ds(4096, 128)], wide.at[pl.ds(4096, 128)]),
                (wide_h.at[pl.ds(2048, 2048)], wide.at[pl.ds(2048, 2048)]),
            )
        )
    ]
    for copy in loads:
        copy.start()

    def scatter(source, target, send, recv):
        for i in order:
            dst = jnp.bitwise_xor(e, i)
            if i == 0:
                pltpu.make_async_copy(source(dst), target(e), recv).start()
            else:
                pltpu.make_async_remote_copy(
                    src_ref=source(dst),
                    dst_ref=target(e),
                    send_sem=send,
                    recv_sem=recv,
                    device_id=(dst, l),
                    device_id_type=MESH,
                ).start()

    def wait_bytes(ref, sem):
        pltpu.make_async_copy(ref, ref, sem).wait()

    pi = sort_matrix(False)

    def sorted_rows(arr, gh):
        base = gh * 512
        rhs = jnp.concatenate(
            [x_in[arr, base : base + 256, :], x_in[arr, base + 256 : base + 512, :]], axis=1
        )
        rows = dot(pi, rhs).astype(jnp.bfloat16)
        return rows[:, :128], rows[:, 128:]

    load_l.wait()
    for gh in range(4):
        sides = swap(*sorted_rows(0, gh), 64)
        for e_lo in range(2):
            send_l[:, e_lo, gh * 16 : gh * 16 + 16, :] = sides[e_lo].reshape(16, 16, 128)

    pl.semaphore_wait(barrier, n)
    trade = pltpu.make_async_remote_copy(
        src_ref=vg,
        dst_ref=x_in.at[1],
        send_sem=swap_sem.at[0],
        recv_sem=swap_sem.at[1],
        device_id=sibling,
        device_id_type=MESH,
    )
    trade.start()
    scatter(
        lambda d: send_l.at[lax.div(d, 2), lax.rem(d, 2)],
        lambda s: recv_l.at[s],
        send_sem.at[2],
        recv_sem.at[2],
    )

    trade.wait()
    for g_hi in range(2):
        tiles = quarters((*sorted_rows(1, 2 * g_hi), *sorted_rows(1, 2 * g_hi + 1)))
        at = slice(g_hi * 16, g_hi * 16 + 16)
        for e_lo in range(2):
            for h in range(2):
                send_g[h, :, e_lo, at, :] = tiles[2 * e_lo + h].reshape(16, 16, 128)
    def put_chunk(h):
        scatter(
            lambda d: send_g.at[h, lax.div(d, 2), lax.rem(d, 2)],
            lambda s: recv_g.at[h, s],
            send_sem.at[h],
            recv_sem.at[h],
        )

    put_chunk(0)

    load_part.wait()
    row = part[pl.ds(e, 1), :] & 63
    row = jnp.concatenate([row] * 4, axis=1)
    lane = lax.broadcasted_iota(jnp.int32, (1, 256), 1)
    target = (row >> 5) * 128 + (lane >> 6) * 32 + (row & 31)
    one_hot = jnp.where(lax.broadcasted_iota(jnp.int32, (256, 256), 0) == target, 1.0, 0.0)
    one_hot = one_hot.astype(jnp.bfloat16)

    def outer_stage(arr, h, rhs):
        sign = 1.0 if arr == 0 else -1.0
        for m in range(4):
            base = arr * 1024 + m * 256
            y = dot(wide[base : base + 256, :], rhs).reshape(16, 2, 8, 256)
            y_re, y_im = y[:, 0], y[:, 1]
            cos = tw[0, m * 128 : (m + 1) * 128, :].reshape(16, 8, 256)
            sin = tw[1, m * 128 : (m + 1) * 128, :].reshape(16, 8, 256) * sign
            z_re = cos * y_re + sin * y_im
            z_im = cos * y_im - sin * y_re
            z = jnp.stack([z_re, z_im], axis=1).reshape(4, 4, 16, 256).astype(jnp.bfloat16)
            for g_hi in range(2):
                tiles = quarters([z[:, i, :, g_hi * 128 : g_hi * 128 + 128] for i in range(4)])
                for g4 in range(4):
                    g = 4 * g_hi + g4
                    zz[arr, h, m * 4 : m * 4 + 4, g * 16 : g * 16 + 16, :] = tiles[g4]

    def middle_stage(h):
        def body(j, carry):
            def spectrum(arr):
                rhs = jnp.concatenate([zz[arr, h, 2 * j], zz[arr, h, 2 * j + 1]], axis=1)
                return dot(wide[4096:4224, arr * 128 : arr * 128 + 128], rhs)

            one, two = spectrum(0), spectrum(1)
            l_re, l_im, g_re, g_im = one[:64], one[64:], two[:64], two[64:]
            prod = jnp.concatenate([l_re * g_re - l_im * g_im, l_re * g_im + l_im * g_re], axis=0)
            prod = prod.astype(jnp.bfloat16)
            at = pl.ds(pl.multiple_of(j * 64, 64), 64)
            cos = tw[2, at, :].reshape(8, 8, 256)
            sin = tw[3, at, :].reshape(8, 8, 256)
            for path, s in ((0, sin), (1, -sin)):
                b3 = wide[4096:4224, 256 + path * 128 : 384 + path * 128]
                a = dot(b3, prod).reshape(8, 2, 8, 256)
                a_re, a_im = a[:, 0], a[:, 1]
                b_re = cos * a_re - s * a_im
                b_im = cos * a_im + s * a_re
                b = jnp.stack([b_re, b_im], axis=1).reshape(2, 4, 16, 256).astype(jnp.bfloat16)
                for side in range(2):
                    tiles = quarters([b[:, i, :, side * 128 : side * 128 + 128] for i in range(4)])
                    for low in range(4):
                        bb[path, h, :, 8 * j + 4 * side + low, :, :] = tiles[low]
            return carry

        lax.fori_loop(0, 8, body, 0, unroll=8)

    def last_stage(path, h, m):
        rhs = jnp.concatenate(
            [bb[path, h, 0].reshape(1024, 128), bb[path, h, 1].reshape(1024, 128)], axis=1
        )
        base = 2048 + path * 1024 + m * 256
        k4 = jnp.concatenate(
            [wide[base : base + 256, :], wide[base + 512 : base + 768, :]], axis=1
        )
        return dot(k4, rhs).astype(jnp.bfloat16)

    loads[0].wait()
    loads[1].wait()
    wait_bytes(recv_l, recv_sem.at[2])
    moved = []
    for g_hi in range(2):
        sides = [
            recv_l[:, gh * 16 : gh * 16 + 16, :].reshape(512, 128)
            for gh in (2 * g_hi, 2 * g_hi + 1)
        ]
        moved.append(
            lax.dot_general(
                jnp.concatenate(sides, axis=1),
                one_hot,
                (((1,), (1,)), ((), ())),
                preferred_element_type=jnp.float32,
            ).astype(jnp.bfloat16)
        )
    for h in range(2):
        lanes = slice(h * 128, h * 128 + 128)
        outer_stage(0, h, jnp.concatenate([moved[0][:, lanes], moved[1][:, lanes]], axis=1))
    put_chunk(1)
    loads[2].wait()
    loads[3].wait()

    for h in range(2):
        wait_bytes(recv_g.at[h], recv_sem.at[h])
        sides = [
            recv_g[h, :, g_hi * 16 : g_hi * 16 + 16, :].reshape(512, 128) for g_hi in range(2)
        ]
        outer_stage(1, h, jnp.concatenate(sides, axis=1))
        middle_stage(h)
        for m in range(2):
            x = last_stage(1, h, m)
            for g_hi in range(2):
                outs_g[h, m * 16 : m * 16 + 16, g_hi * 16 : g_hi * 16 + 16, :] = x[
                    :, g_hi * 128 : g_hi * 128 + 128
                ].reshape(16, 16, 128)
        scatter(
            lambda d: outs_g.at[h, d],
            lambda s: relay.at[h, s],
            back_send_sem.at[h],
            back_recv_sem.at[h],
        )

    for m in range(2):
        xs = [last_stage(0, h, m) for h in range(2)]
        for g_hi in range(2):
            lanes = slice(g_hi * 128, g_hi * 128 + 128)
            x = dot(jnp.concatenate([xs[0][:, lanes], xs[1][:, lanes]], axis=1), one_hot)
            x = x.astype(jnp.bfloat16)
            for t in range(2):
                outs_l[m * 16 : m * 16 + 16, g_hi, t * 16 : t * 16 + 16, :] = x[
                    :, t * 128 : t * 128 + 128
                ].reshape(16, 16, 128)
    scatter(
        lambda d: outs_l.at[d],
        lambda s: q.at[pl.ds(0, 2), s],
        back_send_sem.at[2],
        back_recv_sem.at[2],
    )

    hands = []
    for h in range(2):
        wait_bytes(relay.at[h], back_recv_sem.at[h])
        hand = pltpu.make_async_remote_copy(
            src_ref=relay.at[h],
            dst_ref=q.at[2 + h],
            send_sem=relay_send_sem.at[h],
            recv_sem=relay_recv_sem.at[h],
            device_id=sibling,
            device_id_type=MESH,
        )
        hand.start()
        hands.append(hand)
    for h in range(2):
        sent = outs_g.at[h, pl.ds(0, n - 1)]
        wait_bytes(sent, send_sem.at[h])
        wait_bytes(sent, back_send_sem.at[h])
    sent = outs_l.at[pl.ds(0, n - 1)]
    wait_bytes(sent, send_sem.at[2])
    wait_bytes(sent, back_send_sem.at[2])
    for hand in hands:
        hand.wait()
    wait_bytes(q.at[pl.ds(0, 2)], back_recv_sem.at[2])


def post_kernel(q, lesser, greater, rows, out_sem):
    pi = sort_matrix(True)
    stores = []

    def place(path, gh, tiles):
        both = dot(pi, jnp.concatenate(tiles, axis=1))
        rows[path, gh, :256, :] = both[:, :128]
        rows[path, gh, 256:, :] = both[:, 128:]
        out = (lesser, greater)[path]
        stores.append(
            pltpu.make_async_copy(
                rows.at[path, gh], out.at[pl.ds(gh * 512, 512)], out_sem.at[path, gh]
            )
        )
        stores[-1].start()

    for g_hi in range(2):
        at = slice(g_hi * 16, g_hi * 16 + 16)
        tiles = quarters(
            [q[2 + h, :, e_lo, at, :].reshape(256, 128) for e_lo in range(2) for h in range(2)]
        )
        place(1, 2 * g_hi, tiles[:2])
        place(1, 2 * g_hi + 1, tiles[2:])
    for gh in range(4):
        at = slice(gh % 2 * 16, gh % 2 * 16 + 16)
        sides = [q[gh // 2, :, e_lo, at, :].reshape(256, 128) for e_lo in range(2)]
        place(0, gh, swap(*sides, 64))
    for copy in stores:
        copy.wait()


def as_rows(g):
    return g.reshape(64, 2, 16, 128).transpose(0, 2, 1, 3).reshape(2048, 128)


def from_rows(v):
    return v.reshape(64, 16, 2, 128).transpose(0, 2, 1, 3).reshape(64, 2, 2048)


def per_device(g_lesser, g_greater, partner):
    tables = [jnp.asarray(table) for table in constants()]
    hbm = pl.BlockSpec(memory_space=pltpu.HBM)
    bf16 = jnp.bfloat16
    whole, chunks = (32, 64, 128), (2, 32, 32, 128)
    whole_lt, chunks_lt = (16, 2, 64, 128), (2, 16, 2, 32, 128)
    scratch = [
        pltpu.VMEM((2, 2048, 128), bf16),
        pltpu.VMEM((32, 64), jnp.int32),
        pltpu.VMEM(whole_lt, bf16),
        pltpu.VMEM(chunks_lt, bf16),
        pltpu.VMEM(whole, bf16),
        pltpu.VMEM(chunks, bf16),
        pltpu.VMEM((2, 2, 16, 128, 128), bf16),
        pltpu.VMEM((2, 2, 2, 64, 16, 128), bf16),
        pltpu.VMEM((32, 2, 32, 128), bf16),
        pltpu.VMEM(chunks, bf16),
        pltpu.VMEM(chunks, bf16),
    ]
    scratch += [pltpu.VMEM(t.shape, t.dtype) for t in tables]
    scratch += [pltpu.SemaphoreType.DMA((k,)) for k in (6, 2, 3, 3, 3, 3, 2, 2)]
    operands = [as_rows(g_lesser), as_rows(g_greater), partner[0], *tables]
    operands = [pltpu.with_memory_space_constraint(x, pltpu.HBM) for x in operands]
    q = pl.pallas_call(
        main_kernel,
        out_shape=pltpu.VMEM((4, 32, 32, 128), bf16),
        in_specs=[hbm] * 5,
        out_specs=pl.BlockSpec(memory_space=pl.ANY),
        scratch_shapes=scratch,
        compiler_params=pltpu.CompilerParams(
            collective_id=0, has_side_effects=True, vmem_limit_bytes=MAIN_VMEM
        ),
    )(*operands)
    lesser, greater = pl.pallas_call(
        post_kernel,
        out_shape=[jax.ShapeDtypeStruct((2048, 128), jnp.float32)] * 2,
        in_specs=[pl.BlockSpec(memory_space=pltpu.VMEM)],
        out_specs=[hbm] * 2,
        scratch_shapes=[
            pltpu.VMEM((2, 4, 512, 128), jnp.float32),
            pltpu.SemaphoreType.DMA((2, 4)),
        ],
        compiler_params=pltpu.CompilerParams(vmem_limit_bytes=POST_VMEM),
    )(q.reshape(4, 16, 2, 32, 128))
    return from_rows(lesser), from_rows(greater)


def solution(mesh):
    in_specs = (P("energy", None, "elem"), P("energy", None, "elem"), P("elem", None, None))
    out_specs = (P("energy", None, "elem"), P("energy", None, "elem"))
    return jax.shard_map(
        per_device, mesh=mesh, in_specs=in_specs, out_specs=out_specs, check_vma=False
    )
```

```python
import functools
import math

import jax
import jax.numpy as jnp
import ml_dtypes
import numpy as np
from jax import lax
from jax.experimental import pallas as pl
from jax.experimental.pallas import tpu as pltpu
from jax.sharding import PartitionSpec as P

NE = 2048
NT = 4096
MESH = pl.DeviceIdType.MESH
BF16 = ml_dtypes.bfloat16
MAIN_VMEM = 60 * 1024 * 1024
POST_VMEM = 32 * 1024 * 1024


def rotation(rows, cols, length, sign):
    theta = np.outer(rows, cols) % length * (2.0 * math.pi / length)
    cos, sin = np.cos(theta), sign * np.sin(theta)
    return np.stack([np.stack([cos, -sin], -1), np.stack([sin, cos], -1)], 1)


def widen(small):
    a, _, b, _ = small.shape
    full = np.einsum("acbd,rs->acrbds", small, np.eye(8))
    return full.reshape(a * 16, b * 16).astype(BF16)


@functools.cache
def constants():
    n = np.arange(64)
    half = np.arange(32)
    k1 = np.stack([widen(rotation(n, half, 64, s)) for s in (-1, 1)])
    a2 = []
    for s in (-1, 1):
        m = rotation(n, n, 64, s).transpose(1, 0, 2, 3).reshape(2, 64, 8, 8, 2)
        a2.append(m.transpose(0, 1, 2, 4, 3).reshape(128, 128))
    a2 = np.stack(a2).astype(BF16)
    b3 = []
    for s in (1, -1):
        m = rotation(n, n, 64, s).reshape(8, 8, 2, 64, 2)
        b3.append(m.transpose(0, 2, 1, 4, 3).reshape(128, 128))
    b3 = np.concatenate(b3).astype(BF16)
    k4 = []
    for s in (1, -1):
        m = rotation(half, n, 64, s)
        m = np.stack([m[:, 1], -m[:, 0]], 1)
        k4.append(widen(m))
    k4 = np.stack(k4)
    theta = np.outer(n, n) * (2.0 * math.pi / NT)
    tw = np.stack([np.cos(theta), np.sin(theta)])
    t1 = tw.reshape(2, 64, 8, 8).transpose(0, 1, 3, 2)
    t1 = np.repeat(t1.reshape(2, 512, 8), 32, axis=2).astype(np.float32)
    t3 = tw / (NT * math.sqrt(NE))
    t3 = t3.reshape(2, 8, 8, 64).transpose(0, 1, 3, 2)
    t3 = np.repeat(t3, 32, axis=3).astype(np.float32)
    k4 = k4.reshape(2, 512, 2, 512).transpose(0, 2, 1, 3).reshape(2048, 512)
    small = np.concatenate([a2[0], a2[1], b3[:128], b3[128:]], axis=1)
    wide = np.concatenate([k1.reshape(2048, 512), k4, small])
    return wide, np.concatenate([t1.reshape(2, 512, 256), t3.reshape(2, 512, 256)])


def far_first():
    hops = (0, 1, 2, 1)
    return sorted(range(32), key=lambda i: -(hops[i >> 3] + hops[(i >> 1) & 3] + (i & 1)))


def dot(a, b):
    return jnp.dot(a, b, preferred_element_type=jnp.float32)


def swap(a, b, width):
    axis = a.ndim - 1
    even = (lax.broadcasted_iota(jnp.int32, a.shape, axis) & width) == 0
    first = jnp.where(even, a, pltpu.roll(b, width, axis))
    second = jnp.where(even, pltpu.roll(a, 128 - width, axis), b)
    return first, second


def quarters(tiles):
    p0, p2 = swap(tiles[0], tiles[2], 64)
    p1, p3 = swap(tiles[1], tiles[3], 64)
    return (*swap(p0, p1, 32), *swap(p2, p3, 32))


def sort_matrix(back):
    one = lax.broadcasted_iota(jnp.int32, (256, 256), 0)
    two = lax.broadcasted_iota(jnp.int32, (256, 256), 1)
    if back:
        one, two = two, one
    hit = ((one >> 3) == (two & 31)) & ((one & 7) == (two >> 5))
    return jnp.where(hit, 1.0, 0.0).astype(jnp.bfloat16)


def main_kernel(
    vl, vg, part_h, wide_h, tw_h,
    q,
    x_in, part, send_l, send_g, recv_l, recv_g, zz, bb, outs_l, outs_g, relay, wide, tw,
    in_sem, swap_sem, send_sem, recv_sem, back_send_sem, back_recv_sem, relay_send_sem, relay_recv_sem,
):
    e = lax.axis_index("energy")
    l = lax.axis_index("elem")
    sibling = (e, l + 1 - 2 * lax.rem(l, 2))
    order = far_first()
    n = len(order)
    barrier = pltpu.get_barrier_semaphore()

    load_l = pltpu.make_async_copy(vl, x_in.at[0], in_sem.at[0])
    load_part = pltpu.make_async_copy(part_h, part, in_sem.at[1])
    load_l.start()
    load_part.start()

    def greet(i, carry):
        pl.semaphore_signal(
            barrier, inc=1, device_id=(lax.rem(e + i, n), l), device_id_type=MESH
        )
        return carry

    pl.semaphore_signal(barrier, inc=1, device_id=sibling, device_id_type=MESH)
    lax.fori_loop(1, n, greet, 0)

    loads = [
        pltpu.make_async_copy(src, dst, in_sem.at[2 + i])
        for i, (src, dst) in enumerate(
            (
                (wide_h.at[pl.ds(0, 2048)], wide.at[pl.ds(0, 2048)]),
                (tw_h, tw),
                (wide_h.at[pl.ds(4096, 128)], wide.at[pl.ds(4096, 128)]),
                (wide_h.at[pl.ds(2048, 2048)], wide.at[pl.ds(2048, 2048)]),
            )
        )
    ]
    for copy in loads:
        copy.start()

    def scatter(source, target, send, recv):
        for i in order:
            dst = jnp.bitwise_xor(e, i)
            if i == 0:
                pltpu.make_async_copy(source(dst), target(e), recv).start()
            else:
                pltpu.make_async_remote_copy(
                    src_ref=source(dst),
                    dst_ref=target(e),
                    send_sem=send,
                    recv_sem=recv,
                    device_id=(dst, l),
                    device_id_type=MESH,
                ).start()

    def wait_bytes(ref, sem):
        pltpu.make_async_copy(ref, ref, sem).wait()

    pi = sort_matrix(False)

    def sorted_rows(arr, gh):
        base = gh * 512
        rhs = jnp.concatenate(
            [x_in[arr, base : base + 256, :], x_in[arr, base + 256 : base + 512, :]], axis=1
        )
        rows = dot(pi, rhs).astype(jnp.bfloat16)
        return rows[:, :128], rows[:, 128:]

    load_l.wait()
    for gh in range(4):
        sides = swap(*sorted_rows(0, gh), 64)
        for e_lo in range(2):
            send_l[:, e_lo, gh * 16 : gh * 16 + 16, :] = sides[e_lo].reshape(16, 16, 128)

    pl.semaphore_wait(barrier, n)
    trade = pltpu.make_async_remote_copy(
        src_ref=vg,
        dst_ref=x_in.at[1],
        send_sem=swap_sem.at[0],
        recv_sem=swap_sem.at[1],
        device_id=sibling,
        device_id_type=MESH,
    )
    trade.start()
    scatter(
        lambda d: send_l.at[lax.div(d, 2), lax.rem(d, 2)],
        lambda s: recv_l.at[s],
        send_sem.at[2],
        recv_sem.at[2],
    )

    trade.wait()
    for g_hi in range(2):
        tiles = quarters((*sorted_rows(1, 2 * g_hi), *sorted_rows(1, 2 * g_hi + 1)))
        at = slice(g_hi * 16, g_hi * 16 + 16)
        for e_lo in range(2):
            for h in range(2):
                send_g[h, :, e_lo, at, :] = tiles[2 * e_lo + h].reshape(16, 16, 128)
    def put_chunk(h):
        scatter(
            lambda d: send_g.at[h, lax.div(d, 2), lax.rem(d, 2)],
            lambda s: recv_g.at[h, s],
            send_sem.at[h],
            recv_sem.at[h],
        )

    put_chunk(0)

    load_part.wait()
    row = part[pl.ds(e, 1), :] & 63
    row = jnp.concatenate([row] * 4, axis=1)
    lane = lax.broadcasted_iota(jnp.int32, (1, 256), 1)
    target = (row >> 5) * 128 + (lane >> 6) * 32 + (row & 31)
    one_hot = jnp.where(lax.broadcasted_iota(jnp.int32, (256, 256), 0) == target, 1.0, 0.0)
    one_hot = one_hot.astype(jnp.bfloat16)

    def outer_stage(arr, h, rhs):
        sign = 1.0 if arr == 0 else -1.0
        for m in range(4):
            base = arr * 1024 + m * 256
            y = dot(wide[base : base + 256, :], rhs).reshape(16, 2, 8, 256)
            y_re, y_im = y[:, 0], y[:, 1]
            cos = tw[0, m * 128 : (m + 1) * 128, :].reshape(16, 8, 256)
            sin = tw[1, m * 128 : (m + 1) * 128, :].reshape(16, 8, 256) * sign
            z_re = cos * y_re + sin * y_im
            z_im = cos * y_im - sin * y_re
            z = jnp.stack([z_re, z_im], axis=1).reshape(4, 4, 16, 256).astype(jnp.bfloat16)
            for g_hi in range(2):
                tiles = quarters([z[:, i, :, g_hi * 128 : g_hi * 128 + 128] for i in range(4)])
                for g4 in range(4):
                    g = 4 * g_hi + g4
                    zz[arr, h, m * 4 : m * 4 + 4, g * 16 : g * 16 + 16, :] = tiles[g4]

    def middle_stage(h):
        def body(j, carry):
            def spectrum(arr):
                rhs = jnp.concatenate([zz[arr, h, 2 * j], zz[arr, h, 2 * j + 1]], axis=1)
                return dot(wide[4096:4224, arr * 128 : arr * 128 + 128], rhs)

            one, two = spectrum(0), spectrum(1)
            l_re, l_im, g_re, g_im = one[:64], one[64:], two[:64], two[64:]
            prod = jnp.concatenate([l_re * g_re - l_im * g_im, l_re * g_im + l_im * g_re], axis=0)
            prod = prod.astype(jnp.bfloat16)
            at = pl.ds(pl.multiple_of(j * 64, 64), 64)
            cos = tw[2, at, :].reshape(8, 8, 256)
            sin = tw[3, at, :].reshape(8, 8, 256)
            for path, s in ((0, sin), (1, -sin)):
                b3 = wide[4096:4224, 256 + path * 128 : 384 + path * 128]
                a = dot(b3, prod).reshape(8, 2, 8, 256)
                a_re, a_im = a[:, 0], a[:, 1]
                b_re = cos * a_re - s * a_im
                b_im = cos * a_im + s * a_re
                b = jnp.stack([b_re, b_im], axis=1).reshape(2, 4, 16, 256).astype(jnp.bfloat16)
                for side in range(2):
                    tiles = quarters([b[:, i, :, side * 128 : side * 128 + 128] for i in range(4)])
                    for low in range(4):
                        bb[path, h, :, 8 * j + 4 * side + low, :, :] = tiles[low]
            return carry

        lax.fori_loop(0, 8, body, 0, unroll=8)

    def last_stage(path, h, m):
        rhs = jnp.concatenate(
            [bb[path, h, 0].reshape(1024, 128), bb[path, h, 1].reshape(1024, 128)], axis=1
        )
        base = 2048 + path * 1024 + m * 256
        k4 = jnp.concatenate(
            [wide[base : base + 256, :], wide[base + 512 : base + 768, :]], axis=1
        )
        return dot(k4, rhs).astype(jnp.bfloat16)

    loads[0].wait()
    loads[1].wait()
    wait_bytes(recv_l, recv_sem.at[2])
    moved = []
    for g_hi in range(2):
        sides = [
            recv_l[:, gh * 16 : gh * 16 + 16, :].reshape(512, 128)
            for gh in (2 * g_hi, 2 * g_hi + 1)
        ]
        moved.append(
            lax.dot_general(
                jnp.concatenate(sides, axis=1),
                one_hot,
                (((1,), (1,)), ((), ())),
                preferred_element_type=jnp.float32,
            ).astype(jnp.bfloat16)
        )

    def lesser_stage(h):
        lanes = slice(h * 128, h * 128 + 128)
        outer_stage(0, h, jnp.concatenate([moved[0][:, lanes], moved[1][:, lanes]], axis=1))

    lesser_stage(0)
    put_chunk(1)
    loads[2].wait()
    loads[3].wait()

    for h in range(2):
        wait_bytes(recv_g.at[h], recv_sem.at[h])
        sides = [
            recv_g[h, :, g_hi * 16 : g_hi * 16 + 16, :].reshape(512, 128) for g_hi in range(2)
        ]
        outer_stage(1, h, jnp.concatenate(sides, axis=1))
        middle_stage(h)
        for m in range(2):
            x = last_stage(1, h, m)
            for g_hi in range(2):
                outs_g[h, m * 16 : m * 16 + 16, g_hi * 16 : g_hi * 16 + 16, :] = x[
                    :, g_hi * 128 : g_hi * 128 + 128
                ].reshape(16, 16, 128)
        scatter(
            lambda d: outs_g.at[h, d],
            lambda s: relay.at[h, s],
            back_send_sem.at[h],
            back_recv_sem.at[h],
        )
        if h == 0:
            lesser_stage(1)

    for m in range(2):
        xs = [last_stage(0, h, m) for h in range(2)]
        for g_hi in range(2):
            lanes = slice(g_hi * 128, g_hi * 128 + 128)
            x = dot(jnp.concatenate([xs[0][:, lanes], xs[1][:, lanes]], axis=1), one_hot)
            x = x.astype(jnp.bfloat16)
            for t in range(2):
                outs_l[m * 16 : m * 16 + 16, g_hi, t * 16 : t * 16 + 16, :] = x[
                    :, t * 128 : t * 128 + 128
                ].reshape(16, 16, 128)
    scatter(
        lambda d: outs_l.at[d],
        lambda s: q.at[pl.ds(0, 2), s],
        back_send_sem.at[2],
        back_recv_sem.at[2],
    )

    hands = []
    for h in range(2):
        wait_bytes(relay.at[h], back_recv_sem.at[h])
        hand = pltpu.make_async_remote_copy(
            src_ref=relay.at[h],
            dst_ref=q.at[2 + h],
            send_sem=relay_send_sem.at[h],
            recv_sem=relay_recv_sem.at[h],
            device_id=sibling,
            device_id_type=MESH,
        )
        hand.start()
        hands.append(hand)
    for h in range(2):
        sent = outs_g.at[h, pl.ds(0, n - 1)]
        wait_bytes(sent, send_sem.at[h])
        wait_bytes(sent, back_send_sem.at[h])
    sent = outs_l.at[pl.ds(0, n - 1)]
    wait_bytes(sent, send_sem.at[2])
    wait_bytes(sent, back_send_sem.at[2])
    for hand in hands:
        hand.wait()
    wait_bytes(q.at[pl.ds(0, 2)], back_recv_sem.at[2])


def post_kernel(q, lesser, greater, rows, out_sem):
    pi = sort_matrix(True)
    stores = []

    def place(path, gh, tiles):
        both = dot(pi, jnp.concatenate(tiles, axis=1))
        rows[path, gh, :256, :] = both[:, :128]
        rows[path, gh, 256:, :] = both[:, 128:]
        out = (lesser, greater)[path]
        stores.append(
            pltpu.make_async_copy(
                rows.at[path, gh], out.at[pl.ds(gh * 512, 512)], out_sem.at[path, gh]
            )
        )
        stores[-1].start()

    for g_hi in range(2):
        at = slice(g_hi * 16, g_hi * 16 + 16)
        tiles = quarters(
            [q[2 + h, :, e_lo, at, :].reshape(256, 128) for e_lo in range(2) for h in range(2)]
        )
        place(1, 2 * g_hi, tiles[:2])
        place(1, 2 * g_hi + 1, tiles[2:])
    for gh in range(4):
        at = slice(gh % 2 * 16, gh % 2 * 16 + 16)
        sides = [q[gh // 2, :, e_lo, at, :].reshape(256, 128) for e_lo in range(2)]
        place(0, gh, swap(*sides, 64))
    for copy in stores:
        copy.wait()


def as_rows(g):
    return g.reshape(64, 2, 16, 128).transpose(0, 2, 1, 3).reshape(2048, 128)


def from_rows(v):
    return v.reshape(64, 16, 2, 128).transpose(0, 2, 1, 3).reshape(64, 2, 2048)


def per_device(g_lesser, g_greater, partner):
    tables = [jnp.asarray(table) for table in constants()]
    hbm = pl.BlockSpec(memory_space=pltpu.HBM)
    bf16 = jnp.bfloat16
    whole, chunks = (32, 64, 128), (2, 32, 32, 128)
    whole_lt, chunks_lt = (16, 2, 64, 128), (2, 16, 2, 32, 128)
    scratch = [
        pltpu.VMEM((2, 2048, 128), bf16),
        pltpu.VMEM((32, 64), jnp.int32),
        pltpu.VMEM(whole_lt, bf16),
        pltpu.VMEM(chunks_lt, bf16),
        pltpu.VMEM(whole, bf16),
        pltpu.VMEM(chunks, bf16),
        pltpu.VMEM((2, 2, 16, 128, 128), bf16),
        pltpu.VMEM((2, 2, 2, 64, 16, 128), bf16),
        pltpu.VMEM((32, 2, 32, 128), bf16),
        pltpu.VMEM(chunks, bf16),
        pltpu.VMEM(chunks, bf16),
    ]
    scratch += [pltpu.VMEM(t.shape, t.dtype) for t in tables]
    scratch += [pltpu.SemaphoreType.DMA((k,)) for k in (6, 2, 3, 3, 3, 3, 2, 2)]
    operands = [as_rows(g_lesser), as_rows(g_greater), partner[0], *tables]
    operands = [pltpu.with_memory_space_constraint(x, pltpu.HBM) for x in operands]
    q = pl.pallas_call(
        main_kernel,
        out_shape=pltpu.VMEM((4, 32, 32, 128), bf16),
        in_specs=[hbm] * 5,
        out_specs=pl.BlockSpec(memory_space=pl.ANY),
        scratch_shapes=scratch,
        compiler_params=pltpu.CompilerParams(
            collective_id=0, has_side_effects=True, vmem_limit_bytes=MAIN_VMEM
        ),
    )(*operands)
    lesser, greater = pl.pallas_call(
        post_kernel,
        out_shape=[jax.ShapeDtypeStruct((2048, 128), jnp.float32)] * 2,
        in_specs=[pl.BlockSpec(memory_space=pltpu.VMEM)],
        out_specs=[hbm] * 2,
        scratch_shapes=[
            pltpu.VMEM((2, 4, 512, 128), jnp.float32),
            pltpu.SemaphoreType.DMA((2, 4)),
        ],
        compiler_params=pltpu.CompilerParams(vmem_limit_bytes=POST_VMEM),
    )(q.reshape(4, 16, 2, 32, 128))
    return from_rows(lesser), from_rows(greater)


def solution(mesh):
    in_specs = (P("energy", None, "elem"), P("energy", None, "elem"), P("elem", None, None))
    out_specs = (P("energy", None, "elem"), P("energy", None, "elem"))
    return jax.shard_map(
        per_device, mesh=mesh, in_specs=in_specs, out_specs=out_specs, check_vma=False
    )
```
